128 devices in a mesh: lon: 16 (over y, x_lo, core), ens: 8 (over x_hi, z).
Axes of the slice: x: 4 (x_hi: 2, x_lo: 2; x = x_hi * 2 + x_lo), y: 4, z: 4, core: 2. Of those that a mesh axis runs over, the one named last changes fastest.
Arguments:
- members_in: bfloat16 [8, 64, 8, 4096], P('ens', None, None, 'lon'), may hold values from -6 to 6
- cotangent: bfloat16 [8, 64, 8, 4096], P('ens', None, None, 'lon'), may hold values from -6 to 6
- conv_weight: bfloat16 [4, 64, 576], replicated, may hold values from -0.25 to 0.25
- expand_weight: bfloat16 [4, 256, 64], replicated, may hold values from -0.75 to 0.75
- expand_bias: float32 [4, 256], replicated, may hold values from -3 to 3
- project_weight: bfloat16 [4, 64, 256], replicated, may hold values from -0.375 to 0.375
- orient: int32 [16], replicated, may hold values from 0 to 1
Outputs:
- section_out: bfloat16 [8, 64, 8, 4096], P('ens', None, None, 'lon')
- input_grad: bfloat16 [8, 64, 8, 4096], P('ens', None, None, 'lon')
- conv_grad: float32 [4, 64, 576], P(None, 'ens')
- expand_grad: float32 [4, 256, 64], P(None, 'ens')
- project_grad: float32 [4, 64, 256], P(None, 'ens')
The draws below stay inside these ranges and needn't reach their ends.
Inputs may be any that keep to these rules, and one draw needn't show every extreme that they name: `orient`: 1 where a sector stores its latitude rows in reversed order.
All inputs are finite; a program needn't handle non-finite values.
Results may differ from the reference program's by a relative error of at most 0.034.
Values may be sent and summed in bfloat16 or wider, within the bound.
No kernel may reach another device: no remote copies, remote signals or barrier semaphores. Data moves between devices by JAX's collectives and lax.ppermute only.
A program may use at most 128 MiB of HBM per device.

```python
import jax
import jax.numpy as jnp
from jax import lax

C = 64
HID = 256
H = 8
WD = 256
DEPTH = 4
KC = 576
MEMBERS = 8
SECTORS = 16
WTOT = 4096


def set_ends(entries, rng, low, top_value):
    longest = entries.shape.index(max(entries.shape))
    spots = []
    for shift in (0, 1):
        where = [jax.random.randint(jax.random.fold_in(rng, axis), (), 0, length) for axis, length in enumerate(entries.shape)]
        where[longest] = (where[longest] + shift) % entries.shape[longest]
        spots.append(tuple(where))
    return entries.at[spots[0]].set(low).at[spots[1]].set(top_value)


def raised(drawn, rng, source, target, parts, factor):
    owner, partner = [(jnp.arange(drawn.shape[dim]) // (drawn.shape[dim] // parts)).reshape([-1 if axis == dim else 1 for axis in range(drawn.ndim)]) for dim in (source, target)]
    chosen = jax.random.permutation(rng, parts)[partner]
    strong = (owner == chosen) | (owner == (partner + parts // 2) % parts)
    return jnp.where(strong, factor * drawn, drawn)


def block_levels(stream_key, shape, shards, least, top_value):
    gain = 1.0
    for axis_at, blocks in shards:
        steps = jax.random.uniform(jax.random.fold_in(jax.random.fold_in(stream_key, 6), axis_at), (blocks,), jnp.float32, least / len(shards), top_value / len(shards))
        gain = gain * jnp.repeat(jnp.exp(steps), shape[axis_at] // blocks).reshape((-1,) + (1,) * (len(shape) - 1 - axis_at))
    return gain


def noise(own_key, extent, scale, most, split=(), kind=jnp.bfloat16):
    drawn = scale * jax.random.normal(own_key, extent, jnp.float32)
    if split:
        drawn = drawn * block_levels(own_key, extent, split, -0.22, 0.18)
    return jnp.clip(drawn, -most, most).astype(kind)


def gaussian_with(own_key, dims, spread, bound, pieces, heavy, kind=jnp.bfloat16):
    values = spread * jax.random.normal(own_key, dims, jnp.float32)
    if pieces:
        values = values * block_levels(own_key, dims, pieces, -0.22, 0.18)
    return jnp.clip(raised(values, jax.random.fold_in(own_key, 3), *heavy), -bound, bound).astype(kind)


def setup_inputs(seed: int = 0) -> dict:
    splits = jax.random.split(jax.random.key(seed), 8)
    members_in = noise(splits[0], (MEMBERS, C, H, WTOT), 1.0, 6.0, ((0, 8), (3, 16)))
    cotangent = gaussian_with(splits[1], (MEMBERS, C, H, WTOT), 1.0, 6.0, ((0, 8), (3, 16)), (0, 1, 8, 2.0))
    conv_weight = noise(splits[2], (DEPTH, C, KC), KC ** -0.5, 0.25)
    expand_weight = noise(splits[3], (DEPTH, HID, C), C ** -0.5, 0.75)
    expand_bias = noise(splits[4], (DEPTH, HID), 0.5, 3.0, (), jnp.float32)
    project_weight = noise(splits[5], (DEPTH, C, HID), HID ** -0.5, 0.375)
    orient = set_ends(jax.random.randint(splits[6], (SECTORS,), 0, 2), jax.random.fold_in(splits[6], 1), 0, 1).astype(jnp.int32)
    return {"members_in": members_in, "cotangent": cotangent, "conv_weight": conv_weight, "expand_weight": expand_weight, "expand_bias": expand_bias, "project_weight": project_weight, "orient": orient}


SQRT_HALF = 0.7071067811865476
INV_ROOT_TAU = 0.3989422804014327

def gelu_curve(value):
    return 0.5 * value * (1.0 + jax.scipy.special.erf(value * SQRT_HALF))

def gelu_slope(value):
    return 0.5 * (1.0 + jax.scipy.special.erf(value * SQRT_HALF)) + value * INV_ROOT_TAU * jnp.exp(-0.5 * value * value)

def pad_rows(block):
    return jnp.pad(block, ((0, 0), (1, 1), (0, 0)))

def wrap_cols(block):
    return jnp.concatenate([block[:, :, -1:], block, block[:, :, :1]], axis=2)

def outer_sum(left, right):
    return lax.dot_general(left, right, (((1,), (1,)), ((), ())), preferred_element_type=jnp.float32)

def conv_forward(padded, kernel, count_rows, count_cols):
    channels = kernel.shape[0]
    running = jnp.zeros((channels, count_rows * count_cols), jnp.float32)
    for row_step in range(3):
        for col_step in range(3):
            offset = 3 * row_step + col_step
            window = padded[:, row_step:row_step + count_rows, col_step:col_step + count_cols].reshape(channels, -1)
            running = running + jnp.dot(kernel[:, offset * channels:(offset + 1) * channels], window, preferred_element_type=jnp.float32)
    return running

def conv_transpose(padded, kernel, count_rows, count_cols):
    channels = kernel.shape[0]
    running = jnp.zeros((channels, count_rows * count_cols), jnp.float32)
    for row_step in range(3):
        for col_step in range(3):
            offset = 3 * row_step + col_step
            window = padded[:, 2 - row_step:2 - row_step + count_rows, 2 - col_step:2 - col_step + count_cols].reshape(channels, -1)
            running = running + jnp.dot(kernel[:, offset * channels:(offset + 1) * channels].T, window, preferred_element_type=jnp.float32)
    return running

def kernel_grad(slope, padded, count_rows, count_cols):
    channels = slope.shape[0]
    terms = []
    for row_step in range(3):
        for col_step in range(3):
            window = padded[:, row_step:row_step + count_rows, col_step:col_step + count_cols].reshape(channels, -1)
            terms.append(outer_sum(slope, window))
    return jnp.concatenate(terms, axis=1)

def block_forward(field_flat, padded, kernel, expand, bias, project, count_rows, count_cols):
    hidden = conv_forward(padded, kernel, count_rows, count_cols).astype(jnp.bfloat16)
    inner = jnp.dot(expand, hidden, preferred_element_type=jnp.float32) + bias[:, None]
    active = gelu_curve(inner).astype(jnp.bfloat16)
    output = (field_flat.astype(jnp.float32) + jnp.dot(project, active, preferred_element_type=jnp.float32)).astype(jnp.bfloat16)
    return (hidden, inner, active, output)

def block_backward(upstream, hidden, inner, active, padded, kernel, expand, project, count_rows, count_cols, surround_slope):
    channels = kernel.shape[0]
    d_active = jnp.dot(project.T, upstream, preferred_element_type=jnp.float32)
    d_inner = (d_active * gelu_slope(inner)).astype(jnp.bfloat16)
    project_term = outer_sum(upstream, active)
    expand_term = outer_sum(d_inner, hidden)
    d_hidden = jnp.dot(expand.T, d_inner, preferred_element_type=jnp.float32).astype(jnp.bfloat16)
    kernel_term = kernel_grad(d_hidden, padded, count_rows, count_cols)
    widened = surround_slope(d_hidden.reshape(channels, count_rows, count_cols))
    d_field = (upstream.astype(jnp.float32) + conv_transpose(widened, kernel, count_rows, count_cols)).astype(jnp.bfloat16)
    return (d_field, kernel_term, expand_term, project_term)

def reference(members_in, cotangent, conv_weight, expand_weight, expand_bias, project_weight, orient):
    columns = jnp.arange(WTOT, dtype=jnp.int32) // WD
    flipped = (jnp.take(orient, columns) == 1)[None, None, :]

    def to_frame(block):
        return jnp.where(flipped, block[:, ::-1, :], block)

    def surround(block):
        return pad_rows(wrap_cols(block))

    def member(member_pair):
        field = to_frame(member_pair[0])
        channels = field.shape[0]
        saved = []
        for block_index in range(DEPTH):
            padded = surround(field)
            hidden, inner, active, output = block_forward(field.reshape(channels, -1), padded, conv_weight[block_index], expand_weight[block_index], expand_bias[block_index], project_weight[block_index], H, WTOT)
            saved.append((padded, hidden, inner, active))
            field = output.reshape(channels, H, WTOT)
        upstream = to_frame(member_pair[1]).reshape(channels, -1)
        kernel_terms = [None] * DEPTH
        expand_terms = [None] * DEPTH
        project_terms = [None] * DEPTH
        for block_index in reversed(range(DEPTH)):
            padded, hidden, inner, active = saved[block_index]
            upstream, kernel_terms[block_index], expand_terms[block_index], project_terms[block_index] = block_backward(upstream, hidden, inner, active, padded, conv_weight[block_index], expand_weight[block_index], project_weight[block_index], H, WTOT, surround)
        return (to_frame(field), to_frame(upstream.reshape(channels, H, WTOT)), jnp.stack(kernel_terms), jnp.stack(expand_terms), jnp.stack(project_terms))
    final, input_grad, kernel_all, expand_all, project_all = lax.map(member, (members_in, cotangent))
    return (final, input_grad, lax.optimization_barrier(jnp.sum(kernel_all, axis=0)), lax.optimization_barrier(jnp.sum(expand_all, axis=0)), lax.optimization_barrier(jnp.sum(project_all, axis=0)))
```

```python
import functools

import jax
import jax.numpy as jnp
from jax import lax
from jax.experimental import pallas as pl
from jax.experimental.pallas import tpu as pltpu
from jax.sharding import PartitionSpec as P

BF = jnp.bfloat16
F32 = jnp.float32
SQRT_HALF = 0.7071067811865476
INV_ROOT_TAU = 0.3989422804014327

C = 64
HID = 256
H = 8
WD = 256
HALO = 8
PITCH = WD + 2 * HALO
N = H * PITCH
DEPTH = 4
HALVES = WD // 128
SHARE = 40
CHUNKS = [(s, min(256, N - s)) for s in range(0, N, 256)]
VMEM = 56 * 1024 * 1024

NT = (((1,), (1,)), ((), ()))


def mm(a, b):
    return jnp.dot(a, b, preferred_element_type=F32)


def mm_nt(a, b):
    return lax.dot_general(a, b, NT, preferred_element_type=F32)


def call(body, outs, scratch=(), smem=0, total=0, flops=0, **kw):
    specs = [pl.BlockSpec(memory_space=pltpu.SMEM)] * smem
    specs += [pl.BlockSpec(memory_space=pltpu.VMEM)] * (total - smem)
    return pl.pallas_call(
        body,
        out_shape=outs,
        in_specs=specs,
        out_specs=jax.tree.map(lambda _: pl.BlockSpec(memory_space=pltpu.VMEM), outs),
        scratch_shapes=list(scratch),
        compiler_params=pltpu.CompilerParams(vmem_limit_bytes=VMEM),
        cost_estimate=pl.CostEstimate(flops=flops, bytes_accessed=1 << 20, transcendentals=0),
        **kw,
    )


def shape(*dims, dtype=BF):
    return jax.ShapeDtypeStruct(dims, dtype)


def spread(wide, ref):
    for half in range(HALVES):
        part = ref[:, :, 128 * half : 128 * half + 128]
        wide[half] = part.astype(F32).reshape(C * H, 128)


def edge_kernel(flip_ref, field_ref, slope_ref, low_ref, high_ref, wide_f, wide_g):
    flip = flip_ref[0]
    spread(wide_f, field_ref)
    spread(wide_g, slope_ref)
    lane = lax.broadcasted_iota(jnp.int32, (C, 128), 1)
    low = jnp.zeros((C, 128), F32)
    high = jnp.zeros((C, 128), F32)
    for row in range(H):
        stored = jnp.where(flip == 1, H - 1 - row, row)
        for k, wide in ((0, wide_f), (8, wide_g)):
            at = 16 * row + k
            inside = (lane >= at) & (lane < at + 8)
            first = wide[0, pl.ds(stored, C, stride=H), :]
            last = wide[HALVES - 1, pl.ds(stored, C, stride=H), :]
            low = jnp.where(inside, pltpu.roll(first, at, axis=1), low)
            high = jnp.where(inside, pltpu.roll(last, (at + 8) % 128, axis=1), high)
    low_ref[...] = low.astype(BF)
    high_ref[...] = high.astype(BF)


def flatten(ref, left, right, k, wide, flip):
    spread(wide, ref)
    parts = []
    for row in range(H):
        stored = jnp.where(flip == 1, H - 1 - row, row)
        at = 16 * row + k
        parts.append(left[:, at : at + 8])
        for half in range(HALVES):
            parts.append(wide[half, pl.ds(stored, C, stride=H), :])
        parts.append(right[:, at : at + 8])
    return jnp.concatenate(parts, axis=1)


def unflatten(flat, ref, wide, flip):
    for row in range(H):
        stored = jnp.where(flip == 1, H - 1 - row, row)
        for half in range(HALVES):
            at = row * PITCH + HALO + 128 * half
            wide[half, pl.ds(stored, C, stride=H), :] = flat[:, at : at + 128]
    for half in range(HALVES):
        ref[:, :, 128 * half : 128 * half + 128] = wide[half].reshape(C, H, 128).astype(BF)


def shift(flat, amount):
    return pltpu.roll(flat, amount % N, axis=1)


def rows_stack(dst, value, lane, sign):
    before = jnp.where(lane < PITCH, 0, shift(value, PITCH)).astype(BF)
    after = jnp.where(lane >= N - PITCH, 0, shift(value, -PITCH)).astype(BF)
    first, last = (before, after) if sign > 0 else (after, before)
    dst[0:C, :] = first
    dst[C : 2 * C, :] = value
    dst[2 * C : 3 * C, :] = last


def main_kernel(
    flip_ref,
    field_ref,
    slope_ref,
    left_ref,
    right_ref,
    conv_ref,
    convt_ref,
    expand_ref,
    expandt_ref,
    bias_ref,
    project_ref,
    projectt_ref,
    out_ref,
    grad_ref,
    share_ref,
    wide,
    stack_s,
    hid_s,
    wide_s,
    up_s,
    dh_s,
    rstack_s,
    share_s,
):
    flip = flip_ref[0]
    lane = lax.broadcasted_iota(jnp.int32, (C, N), 1)
    column = lane
    for row in range(1, H):
        column = jnp.where(lane >= row * PITCH, lane - row * PITCH, column)
    inside = (column >= HALO) & (column < HALO + WD)
    mask = jnp.where(inside, 1.0, 0.0).astype(BF)
    left = left_ref[...].astype(F32)
    right = right_ref[...].astype(F32)

    field = flatten(field_ref, left, right, 0, wide, flip).astype(BF)
    for b in range(DEPTH):
        rows_stack(stack_s.at[b], field, lane, 1)
        for start, size in CHUNKS:
            cut = slice(start, start + size)
            wide_s[:, cut] = mm(conv_ref[b], stack_s[b, :, cut])
        hid_s[b] = (
            shift(wide_s[0:C, :], 1) + wide_s[C : 2 * C, :] + shift(wide_s[2 * C : 3 * C, :], -1)
        ).astype(BF)
        parts = []
        for start, size in CHUNKS:
            cut = slice(start, start + size)
            inner = mm(expand_ref[b], hid_s[b, :, cut]) + bias_ref[b]
            active = (0.5 * inner * (1.0 + lax.erf(inner * SQRT_HALF))).astype(BF)
            old = stack_s[b, C : 2 * C, cut].astype(F32)
            parts.append((old + mm(project_ref[b], active)).astype(BF))
        field = jnp.concatenate(parts, axis=1)
    unflatten(field.astype(F32), out_ref, wide, flip)

    up_s[...] = flatten(slope_ref, left, right, 8, wide, flip).astype(BF)
    for b in reversed(range(DEPTH)):
        pg = jnp.zeros((C, HID), F32)
        eg = jnp.zeros((HID, C), F32)
        for start, size in CHUNKS:
            cut = slice(start, start + size)
            up = up_s[:, cut]
            hidden = hid_s[b, :, cut]
            d_active = mm(projectt_ref[b], up)
            inner = mm(expand_ref[b], hidden) + bias_ref[b]
            half = 0.5 * (1.0 + lax.erf(inner * SQRT_HALF))
            active = (inner * half).astype(BF)
            slope = half + inner * (INV_ROOT_TAU * jnp.exp(-0.5 * inner * inner))
            d_inner = (d_active * slope).astype(BF)
            dh_s[:, cut] = mm(expandt_ref[b], d_inner).astype(BF)
            pg = pg + mm_nt(up * mask[:, cut], active)
            eg = eg + mm_nt(d_inner, hidden * mask[:, cut])
        d_hidden = dh_s[...]
        rows_stack(rstack_s, d_hidden, lane, -1)
        for start, size in CHUNKS:
            cut = slice(start, start + size)
            wide_s[:, cut] = mm(convt_ref[b], rstack_s[:, cut])
        up_s[...] = (
            up_s[...].astype(F32)
            + (shift(wide_s[0:C, :], -1) + wide_s[C : 2 * C, :] + shift(wide_s[2 * C : 3 * C, :], 1))
        ).astype(BF)
        own = d_hidden * mask
        rstack_s[0:C, :] = shift(own, -1)
        rstack_s[C : 2 * C, :] = own
        rstack_s[2 * C : 3 * C, :] = shift(own, 1)
        cg = mm_nt(rstack_s[...], stack_s[b])
        for e in range(8):
            low = [cg[c * C + 8 * e : c * C + 8 * e + 8, :] for c in range(3)]
            low.append(jnp.zeros((8, 3 * C), F32))
            share_s[e, 0:32, :] = jnp.concatenate(
                [jnp.concatenate(low, axis=0), eg[32 * e : 32 * e + 32, :]], axis=1
            )
            share_s[e, 32:40, :] = pg[8 * e : 8 * e + 8, :]
        share_ref[b] = share_s[...].reshape(8 * SHARE, 256).astype(BF)
    unflatten(up_s[...].astype(F32), grad_ref, wide, flip)


def sum_kernel(parts, rows, src_ref, dst_ref):
    total = src_ref[0].astype(F32)
    for part in range(1, parts):
        total = total + src_ref[part].astype(F32)
    dst_ref[...] = total.astype(dst_ref.dtype)


def unpack_kernel(src_ref, conv_ref, expand_ref, project_ref):
    for b in range(DEPTH):
        total = src_ref[0, b].astype(F32)
        for part in range(1, src_ref.shape[0]):
            total = total + src_ref[part, b].astype(F32)
        pieces = []
        for r in range(3):
            for c in range(3):
                pieces.append(total[8 * c : 8 * c + 8, C * r : C * r + C])
        conv_ref[b] = jnp.concatenate(pieces, axis=1)
        expand_ref[b] = total[0:32, 3 * C : 4 * C]
        project_ref[b] = total[32:40, :]


def local(members_in, cotangent, conv_weight, expand_weight, expand_bias, project_weight, orient):
    count = lax.axis_size("lon")
    sector = lax.axis_index("lon")
    sectors = jnp.arange(orient.shape[0], dtype=jnp.int32)
    flip = jnp.sum(jnp.where(sectors == sector, orient, 0)).reshape(1)
    field = members_in[0]
    slope = cotangent[0]
    low, high = call(
        edge_kernel,
        [shape(C, 128)] * 2,
        [pltpu.VMEM((HALVES, C * H, 128), F32)] * 2,
        smem=1,
        total=3,
    )(flip, field, slope)
    forward = [(i, (i + 1) % count) for i in range(count)]
    backward = [((i + 1) % count, i) for i in range(count)]
    left = lax.ppermute(high, "lon", forward)
    right = lax.ppermute(low, "lon", backward)

    kernels = conv_weight.reshape(DEPTH, C, 3, 3, C)
    conv = kernels.transpose(0, 3, 1, 2, 4).reshape(DEPTH, 3 * C, 3 * C)
    convt = kernels.transpose(0, 3, 4, 2, 1).reshape(DEPTH, 3 * C, 3 * C)
    section_out, input_grad, shares = call(
        main_kernel,
        [shape(C, H, WD), shape(C, H, WD), shape(DEPTH, 8 * SHARE, 256)],
        [
            pltpu.VMEM((HALVES, C * H, 128), F32),
            pltpu.VMEM((DEPTH, 3 * C, N), BF),
            pltpu.VMEM((DEPTH, C, N), BF),
            pltpu.VMEM((3 * C, N), F32),
            pltpu.VMEM((C, N), BF),
            pltpu.VMEM((C, N), BF),
            pltpu.VMEM((3 * C, N), BF),
            pltpu.VMEM((8, SHARE, 256), F32),
        ],
        smem=1,
        total=12,
    )(
        flip,
        field,
        slope,
        left,
        right,
        conv,
        convt,
        expand_weight,
        expand_weight.transpose(0, 2, 1),
        expand_bias[:, :, None],
        project_weight,
        project_weight.transpose(0, 2, 1),
    )
    parts = shares.reshape(DEPTH, 8, SHARE, 256).transpose(1, 0, 2, 3)
    parts = lax.all_to_all(parts, "ens", 0, 0, tiled=True)
    parts = call(functools.partial(sum_kernel, 8, SHARE), shape(DEPTH, SHARE, 256), total=1)(parts)
    parts = jnp.broadcast_to(parts[None], (count, DEPTH, SHARE, 256))
    parts = lax.all_to_all(parts, "lon", 0, 0, tiled=True)
    conv_grad, expand_grad, project_grad = call(
        unpack_kernel,
        [
            shape(DEPTH, 8, 9 * C, dtype=F32),
            shape(DEPTH, 32, C, dtype=F32),
            shape(DEPTH, 8, HID, dtype=F32),
        ],
        total=1,
    )(parts)
    return section_out[None], input_grad[None], conv_grad, expand_grad, project_grad


def solution(mesh):
    cells = P("ens", None, None, "lon")
    rows = P(None, "ens", None)
    return jax.shard_map(
        local,
        mesh=mesh,
        in_specs=(cells, cells, P(), P(), P(), P(), P()),
        out_specs=(cells, cells, rows, rows, rows),
        check_vma=False,
    )
```

```python
import jax
import jax.numpy as jnp
from jax import lax
from jax.experimental import pallas as pl
from jax.experimental.pallas import tpu as pltpu
from jax.sharding import Mesh
from jax.sharding import PartitionSpec as P

BF = jnp.bfloat16
F32 = jnp.float32
SQRT_HALF = 0.7071067811865476
INV_ROOT_TAU = 0.3989422804014327
HALF_LOG2E = 0.7213475204444817

C = 64
HID = 256
H = 8
WD = 256
HALO = 8
PITCH = WD + 2 * HALO
N = H * PITCH
DEPTH = 4
HALVES = WD // 128
TILES = N // 128
UNITS = 72
CHUNKS = [(s, min(256, N - s)) for s in range(0, N, 256)]
VMEM = 56 * 1024 * 1024
LON = ("y", "xl", "core")

NT = (((1,), (1,)), ((), ()))


def mm(a, b):
    return jnp.dot(a, b, preferred_element_type=F32)


def mm_nt(a, b):
    return lax.dot_general(a, b, NT, preferred_element_type=F32)


def call(body, outs, ins, scratch=(), flops=0):
    specs = [
        pl.BlockSpec(memory_space=pltpu.SMEM if scalar else pltpu.VMEM) for _, scalar in ins
    ]
    return pl.pallas_call(
        body,
        out_shape=outs,
        in_specs=specs,
        out_specs=jax.tree.map(lambda _: pl.BlockSpec(memory_space=pltpu.VMEM), outs),
        scratch_shapes=list(scratch),
        compiler_params=pltpu.CompilerParams(vmem_limit_bytes=VMEM),
        cost_estimate=pl.CostEstimate(flops=flops, bytes_accessed=1 << 20, transcendentals=0),
    )(*[array for array, _ in ins])


def shape(*dims, dtype=BF):
    return jax.ShapeDtypeStruct(dims, dtype)


def spread(wide, ref):
    for half in range(HALVES):
        part = ref[:, :, 128 * half : 128 * half + 128]
        wide[half] = part.astype(F32).reshape(C * H, 128)


def stored_row(flip, row):
    return jnp.where(flip == 1, H - 1 - row, row)


def edge_kernel(place_ref, field_ref, slope_ref, low_ref, high_ref, wide_f, wide_g):
    flip = place_ref[0]
    spread(wide_f, field_ref)
    spread(wide_g, slope_ref)
    lane = lax.broadcasted_iota(jnp.int32, (C, 128), 1)
    low = jnp.zeros((C, 128), F32)
    high = jnp.zeros((C, 128), F32)
    for row in range(H):
        stored = stored_row(flip, row)
        for k, wide in ((0, wide_f), (8, wide_g)):
            at = 16 * row + k
            inside = (lane >= at) & (lane < at + 8)
            first = wide[0, pl.ds(stored, C, stride=H), :]
            last = wide[HALVES - 1, pl.ds(stored, C, stride=H), :]
            low = jnp.where(inside, pltpu.roll(first, at, axis=1), low)
            high = jnp.where(inside, pltpu.roll(last, (at + 8) % 128, axis=1), high)
    low_ref[...] = low.astype(BF)
    high_ref[...] = high.astype(BF)


def flatten(ref, wide, flip):
    spread(wide, ref)
    edge = jnp.zeros((C, HALO), F32)
    parts = []
    for row in range(H):
        stored = stored_row(flip, row)
        parts.append(edge)
        for half in range(HALVES):
            parts.append(wide[half, pl.ds(stored, C, stride=H), :])
        parts.append(edge)
    return jnp.concatenate(parts, axis=1)


def unflatten(flat_ref, ref, wide, flip):
    for row in range(H):
        stored = stored_row(flip, row)
        for half in range(HALVES):
            at = row * PITCH + HALO + 128 * half
            wide[half, pl.ds(stored, C, stride=H), :] = flat_ref[:, at : at + 128].astype(F32)
    for half in range(HALVES):
        ref[:, :, 128 * half : 128 * half + 128] = wide[half].reshape(C, H, 128).astype(BF)


def prep_kernel(
    place_ref,
    field_ref,
    slope_ref,
    kernel_ref,
    expandt_ref,
    bias_ref,
    project_ref,
    field_out,
    slope_out,
    conv_out,
    convt_out,
    expand_out,
    projectt_out,
    bias_out,
    wide,
):
    flip = place_ref[0]
    field_out[...] = flatten(field_ref, wide, flip).astype(BF)
    slope_out[...] = flatten(slope_ref, wide, flip).astype(BF)
    for b in range(DEPTH):
        taps = kernel_ref[b]
        turned = taps.astype(F32).T
        for c in range(3):
            here = slice(c * C, c * C + C)
            at = [(3 * r + c) * C for r in range(3)]
            conv_out[b, here, :] = jnp.concatenate([taps[:, a : a + C] for a in at], axis=1)
            convt_out[b, here, :] = jnp.concatenate(
                [turned[a : a + C, :] for a in at], axis=1
            ).astype(BF)
        expand_out[b] = expandt_ref[b].astype(F32).T.astype(BF)
        projectt_out[b] = project_ref[b].astype(F32).T.astype(BF)
        bias_out[b] = jnp.broadcast_to(bias_ref[b : b + 1, :], (128, HID)).T


def add_halo(flat_ref, left, right):
    lane = lax.broadcasted_iota(jnp.int32, (C, 128), 1)
    for j in range(H + 1):
        cut = slice(256 * j, 256 * j + 128)
        tile = flat_ref[:, cut].astype(F32)
        tile = jnp.where((lane >= 16 * j) & (lane < 16 * j + 8), left, tile)
        tile = jnp.where((lane >= 16 * j - 8) & (lane < 16 * j), right, tile)
        flat_ref[:, cut] = tile.astype(BF)


def shift(flat, amount):
    return pltpu.roll(flat, amount % N, axis=1)


def rows_stack(dst, value, lane, sign):
    before = jnp.where(lane < PITCH, 0, shift(value, PITCH)).astype(BF)
    after = jnp.where(lane >= N - PITCH, 0, shift(value, -PITCH)).astype(BF)
    first, last = (before, after) if sign > 0 else (after, before)
    dst[0:C, :] = first
    dst[C : 2 * C, :] = value
    dst[2 * C : 3 * C, :] = last


def conv_pass(dst, weights, src):
    for start, size in CHUNKS:
        cut = slice(start, start + size)
        dst[:, cut] = mm(weights, src[:, cut])


def pack_share(dst, at, cg, eg, pg):
    blank = jnp.zeros((8, C), F32)
    for e in range(8):
        conv = [cg[c * C + 8 * e : c * C + 8 * e + 8, :] for c in range(3)]
        wide = [eg[32 * e + 8 * i : 32 * e + 8 * i + 8, :] for i in range(4)]
        tail = [conv[i][:, 128:192] for i in range(3)] + wide + [blank]
        units = [conv[i][:, 0:128] for i in range(3)]
        units += [pg[8 * e : 8 * e + 8, 0:128], pg[8 * e : 8 * e + 8, 128:256]]
        units += [jnp.concatenate(tail[2 * i : 2 * i + 2], axis=1) for i in range(4)]
        for i, unit in enumerate(units):
            dst[at, e, 8 * i : 8 * i + 8, :] = unit


def main_kernel(
    place_ref,
    field_ref,
    slope_ref,
    left_ref,
    right_ref,
    conv_ref,
    convt_ref,
    expand_ref,
    expandt_ref,
    bias_ref,
    project_ref,
    projectt_ref,
    out_ref,
    up_ref,
    dh_ref,
    own_ref,
    other_ref,
    stack_s,
    hid_s,
    active_s,
    slope_s,
    wide_s,
    rstack_s,
    share_s,
):
    core = place_ref[1]
    lane = lax.broadcasted_iota(jnp.int32, (C, N), 1)
    column = lane
    for row in range(1, H):
        column = jnp.where(lane >= row * PITCH, lane - row * PITCH, column)
    inside = (column >= HALO) & (column < HALO + WD)
    mask = jnp.where(inside, 1.0, 0.0).astype(BF)

    left = left_ref[...].astype(F32)
    right = right_ref[...].astype(F32)
    out_ref[...] = field_ref[...]
    add_halo(out_ref, left, pltpu.roll(right, 8, axis=1))
    up_ref[...] = slope_ref[...]
    add_halo(up_ref, pltpu.roll(left, 120, axis=1), right)

    for b in range(DEPTH):
        rows_stack(stack_s.at[b], out_ref[...], lane, 1)
        conv_pass(wide_s, conv_ref[b], stack_s.at[b])
        hid_s[b] = (
            shift(wide_s[0:C, :], 1) + wide_s[C : 2 * C, :] + shift(wide_s[2 * C : 3 * C, :], -1)
        ).astype(BF)
        for start, size in CHUNKS:
            cut = slice(start, start + size)
            bias = jnp.concatenate([bias_ref[b]] * (size // 128), axis=1)
            inner = mm(expand_ref[b], hid_s[b, :, cut]) + bias
            half = 0.5 + 0.5 * lax.erf(inner * SQRT_HALF)
            active = (inner * half).astype(BF)
            bell = jnp.exp2((inner * inner) * -HALF_LOG2E)
            slope_s[b, :, cut] = (half + (inner * INV_ROOT_TAU) * bell).astype(BF)
            active_s[b, :, cut] = active
            old = out_ref[:, cut].astype(F32)
            out_ref[:, cut] = (old + mm(project_ref[b], active)).astype(BF)

    for b in reversed(range(DEPTH)):
        pg = jnp.zeros((C, HID), F32)
        eg = jnp.zeros((HID, C), F32)
        for start, size in CHUNKS:
            cut = slice(start, start + size)
            up = up_ref[:, cut]
            d_active = mm(projectt_ref[b], up)
            d_inner = (d_active * slope_s[b, :, cut].astype(F32)).astype(BF)
            dh_ref[:, cut] = mm(expandt_ref[b], d_inner).astype(BF)
            pg = pg + mm_nt(up * mask[:, cut], active_s[b, :, cut])
            eg = eg + mm_nt(d_inner, hid_s[b, :, cut] * mask[:, cut])
        own = dh_ref[...] * mask
        rstack_s[0:C, :] = shift(own, -1)
        rstack_s[C : 2 * C, :] = own
        rstack_s[2 * C : 3 * C, :] = shift(own, 1)
        cg = mm_nt(rstack_s[...], stack_s[b])
        pack_share(share_s, b, cg, eg, pg)
        if b > 0:
            step_back(up_ref, dh_ref, convt_ref[b], rstack_s, wide_s, lane)
    own_ref[...] = share_s[pl.ds(2 * core, 2)].reshape(16 * UNITS, 128).astype(BF)
    other_ref[...] = share_s[pl.ds(2 - 2 * core, 2)].reshape(16 * UNITS, 128).astype(BF)


def step_back(up_ref, dh_ref, weights, rstack_s, wide_s, lane):
    rows_stack(rstack_s, dh_ref[...], lane, -1)
    conv_pass(wide_s, weights, rstack_s)
    up_ref[...] = (
        up_ref[...].astype(F32)
        + (shift(wide_s[0:C, :], -1) + wide_s[C : 2 * C, :] + shift(wide_s[2 * C : 3 * C, :], 1))
    ).astype(BF)


def tail_kernel(
    place_ref, flat_ref, up_in, dh_ref, convt_ref, out_ref, grad_ref, wide, up_s, rstack_s, wide_s
):
    flip = place_ref[0]
    lane = lax.broadcasted_iota(jnp.int32, (C, N), 1)
    up_s[...] = up_in[...]
    step_back(up_s, dh_ref, convt_ref[0], rstack_s, wide_s, lane)
    unflatten(flat_ref, out_ref, wide, flip)
    unflatten(up_s, grad_ref, wide, flip)


def pair_kernel(own_ref, other_ref, dst_ref):
    dst_ref[...] = (own_ref[...].astype(F32) + other_ref[...].astype(F32)).astype(BF)


def sum_kernel(src_ref, dst_ref):
    total = src_ref[0].astype(F32)
    for part in range(1, src_ref.shape[0]):
        total = total + src_ref[part].astype(F32)
    total = total.astype(BF)
    for part in range(dst_ref.shape[0]):
        dst_ref[part] = total


def unpack_kernel(src_ref, conv_ref, expand_ref, project_ref):
    for b in range(DEPTH):
        core, xl = b // 2, b % 2
        total = 0.0
        for y in range(4):
            total = total + src_ref[4 * y + 2 * xl + core].astype(F32)
        unit = [total[8 * i : 8 * i + 8, :] for i in range(9)]
        tail = []
        for i in range(5, 9):
            tail += [unit[i][:, 0:C], unit[i][:, C : 2 * C]]
        pieces = []
        for r in range(3):
            for c in range(3):
                pieces.append(tail[c] if r == 2 else unit[c][:, C * r : C * r + C])
        conv_ref[b] = jnp.concatenate(pieces, axis=1)
        for i in range(4):
            expand_ref[b, 8 * i : 8 * i + 8, :] = tail[3 + i]
        project_ref[b] = jnp.concatenate([unit[3], unit[4]], axis=1)


def local(members_in, cotangent, conv_weight, expand_weight, expand_bias, project_weight, orient):
    core = lax.axis_index("core")
    sector = lax.axis_index(LON)
    flip = lax.dynamic_index_in_dim(orient, sector, 0, keepdims=False)
    place = jnp.stack([flip, core])
    field = members_in[0]
    slope = cotangent[0]
    wide = pltpu.VMEM((HALVES, C * H, 128), F32)
    low, high = call(
        edge_kernel,
        [shape(C, 128)] * 2,
        [(place, True), (field, False), (slope, False)],
        [wide, wide],
    )
    count = lax.axis_size(LON)
    left = lax.ppermute(high, LON, [(i, (i + 1) % count) for i in range(count)])
    right = lax.ppermute(low, LON, [((i + 1) % count, i) for i in range(count)])

    expandt = expand_weight.transpose(0, 2, 1)
    flat_f, flat_g, conv, convt, expand, projectt, bias = call(
        prep_kernel,
        [
            shape(C, N),
            shape(C, N),
            shape(DEPTH, 3 * C, 3 * C),
            shape(DEPTH, 3 * C, 3 * C),
            shape(DEPTH, HID, C),
            shape(DEPTH, HID, C),
            shape(DEPTH, HID, 128, dtype=F32),
        ],
        [
            (place, True),
            (field, False),
            (slope, False),
            (conv_weight, False),
            (expandt, False),
            (expand_bias, False),
            (project_weight, False),
        ],
        [wide],
        flops=1 << 27,
    )
    flat_out, up, d_hidden, own, other = call(
        main_kernel,
        [
            shape(C, N),
            shape(C, N),
            shape(C, N),
            shape(16 * UNITS, 128),
            shape(16 * UNITS, 128),
        ],
        [
            (place, True),
            (flat_f, False),
            (flat_g, False),
            (left, False),
            (right, False),
            (conv, False),
            (convt, False),
            (expand, False),
            (expandt, False),
            (bias, False),
            (project_weight, False),
            (projectt, False),
        ],
        [
            pltpu.VMEM((DEPTH, 3 * C, N), BF),
            pltpu.VMEM((DEPTH, C, N), BF),
            pltpu.VMEM((DEPTH, HID, N), BF),
            pltpu.VMEM((DEPTH, HID, N), BF),
            pltpu.VMEM((3 * C, N), F32),
            pltpu.VMEM((3 * C, N), BF),
            pltpu.VMEM((DEPTH, 8, UNITS, 128), F32),
        ],
        flops=1 << 33,
    )
    came = lax.ppermute(other, "core", [(0, 1), (1, 0)])
    share = call(pair_kernel, shape(16 * UNITS, 128), [(own, False), (came, False)])
    parts = lax.all_to_all(share.reshape(16, UNITS, 128), ("xl", "ens"), 0, 0, tiled=True)
    section_out, input_grad = call(
        tail_kernel,
        [shape(C, H, WD)] * 2,
        [(place, True), (flat_out, False), (up, False), (d_hidden, False), (convt, False)],
        [wide, pltpu.VMEM((C, N), BF), pltpu.VMEM((3 * C, N), BF), pltpu.VMEM((3 * C, N), F32)],
        flops=1 << 30,
    )
    parts = call(sum_kernel, shape(count, UNITS, 128), [(parts, False)])
    parts = lax.all_to_all(parts, LON, 0, 0, tiled=True)
    conv_grad, expand_grad, project_grad = call(
        unpack_kernel,
        [
            shape(DEPTH, 8, 9 * C, dtype=F32),
            shape(DEPTH, 32, C, dtype=F32),
            shape(DEPTH, 8, HID, dtype=F32),
        ],
        [(parts, False)],
    )
    return section_out[None], input_grad[None], conv_grad, expand_grad, project_grad


def solution(mesh):
    split = Mesh(mesh.devices.reshape(4, 2, 2, 8), LON + ("ens",))
    cells = P("ens", None, None, LON)
    rows = P(None, "ens", None)
    return jax.shard_map(
        local,
        mesh=split,
        in_specs=(cells, cells, P(), P(), P(), P(), P()),
        out_specs=(cells, cells, rows, rows, rows),
        check_vma=False,
    )
```

```python
import jax
import jax.numpy as jnp
from jax import lax
from jax.experimental import pallas as pl
from jax.experimental.pallas import tpu as pltpu
from jax.sharding import Mesh
from jax.sharding import PartitionSpec as P

BF = jnp.bfloat16
F32 = jnp.float32
SQRT_HALF = 0.7071067811865476
INV_ROOT_TAU = 0.3989422804014327
HALF_LOG2E = 0.7213475204444817

C = 64
HID = 256
H = 8
WD = 256
HALO = 8
PITCH = WD + 2 * HALO
N = H * PITCH
DEPTH = 4
HALVES = WD // 128
TILES = N // 128
UNITS = 72
CHUNKS = [(s, min(256, N - s)) for s in range(0, N, 256)]
FORWARD_LAG = 7
BACKWARD_LAG = 8
TURN = 6
LON = ("y", "xl", "core")

NT = (((1,), (1,)), ((), ()))


def mm(a, b):
    return jnp.dot(a, b, preferred_element_type=F32)


def mm_nt(a, b):
    return lax.dot_general(a, b, NT, preferred_element_type=F32)


def call(body, outs, ins, scratch=(), flops=0, mib=8):
    specs = [
        pl.BlockSpec(memory_space=pltpu.SMEM if scalar else pltpu.VMEM) for _, scalar in ins
    ]
    return pl.pallas_call(
        body,
        out_shape=outs,
        in_specs=specs,
        out_specs=jax.tree.map(lambda _: pl.BlockSpec(memory_space=pltpu.VMEM), outs),
        scratch_shapes=list(scratch),
        compiler_params=pltpu.CompilerParams(vmem_limit_bytes=mib << 20),
        cost_estimate=pl.CostEstimate(flops=flops, bytes_accessed=1 << 20, transcendentals=0),
    )(*[array for array, _ in ins])


def shape(*dims, dtype=BF):
    return jax.ShapeDtypeStruct(dims, dtype)


def spread(wide, ref):
    for half in range(HALVES):
        part = ref[:, :, 128 * half : 128 * half + 128]
        wide[half] = part.astype(F32).reshape(C * H, 128)


def own_flip(orient_ref):
    sector = (lax.axis_index("y") * 2 + lax.axis_index("xl")) * 2 + lax.axis_index("core")
    return orient_ref[sector]


def stored_row(flip, row):
    return jnp.where(flip == 1, H - 1 - row, row)


def edge_kernel(orient_ref, field_ref, slope_ref, low_ref, high_ref, wide_f, wide_g):
    flip = own_flip(orient_ref)
    spread(wide_f, field_ref)
    spread(wide_g, slope_ref)
    lane = lax.broadcasted_iota(jnp.int32, (C, 128), 1)
    low = jnp.zeros((C, 128), F32)
    high = jnp.zeros((C, 128), F32)
    for row in range(H):
        stored = stored_row(flip, row)
        for k, wide in ((0, wide_f), (8, wide_g)):
            at = 16 * row + k
            inside = (lane >= at) & (lane < at + 8)
            first = wide[0, pl.ds(stored, C, stride=H), :]
            last = wide[HALVES - 1, pl.ds(stored, C, stride=H), :]
            low = jnp.where(inside, pltpu.roll(first, at, axis=1), low)
            high = jnp.where(inside, pltpu.roll(last, (at + 8) % 128, axis=1), high)
    low_ref[...] = low.astype(BF)
    high_ref[...] = high.astype(BF)


def flatten(ref, wide, flip):
    spread(wide, ref)
    edge = jnp.zeros((C, HALO), F32)
    parts = []
    for row in range(H):
        stored = stored_row(flip, row)
        parts.append(edge)
        for half in range(HALVES):
            parts.append(wide[half, pl.ds(stored, C, stride=H), :])
        parts.append(edge)
    return jnp.concatenate(parts, axis=1)


def unflatten(flat_ref, ref, wide, flip):
    for row in range(H):
        stored = stored_row(flip, row)
        for half in range(HALVES):
            at = row * PITCH + HALO + 128 * half
            wide[half, pl.ds(stored, C, stride=H), :] = flat_ref[:, at : at + 128].astype(F32)
    for half in range(HALVES):
        ref[:, :, 128 * half : 128 * half + 128] = wide[half].reshape(C, H, 128).astype(BF)


def prep_kernel(
    orient_ref,
    field_ref,
    slope_ref,
    kernel_ref,
    expandt_ref,
    bias_ref,
    project_ref,
    field_out,
    slope_out,
    conv_out,
    convt_out,
    expand_out,
    projectt_out,
    bias_out,
    wide,
):
    flip = own_flip(orient_ref)
    field_out[...] = flatten(field_ref, wide, flip).astype(BF)
    slope_out[...] = flatten(slope_ref, wide, flip).astype(BF)
    for b in range(DEPTH):
        taps = kernel_ref[b]
        turned = taps.astype(F32).T
        for c in range(3):
            here = slice(c * C, c * C + C)
            at = [(3 * r + c) * C for r in range(3)]
            conv_out[b, here, :] = jnp.concatenate([taps[:, a : a + C] for a in at], axis=1)
            convt_out[b, here, :] = jnp.concatenate(
                [turned[a : a + C, :] for a in at], axis=1
            ).astype(BF)
        expand_out[b] = expandt_ref[b].astype(F32).T.astype(BF)
        projectt_out[b] = project_ref[b].astype(F32).T.astype(BF)
        bias_out[b] = jnp.broadcast_to(bias_ref[b : b + 1, :], (128, HID)).T


def add_halo(flat_ref, left, right):
    lane = lax.broadcasted_iota(jnp.int32, (C, 128), 1)
    for j in range(H + 1):
        cut = slice(256 * j, 256 * j + 128)
        tile = flat_ref[:, cut].astype(F32)
        tile = jnp.where((lane >= 16 * j) & (lane < 16 * j + 8), left, tile)
        tile = jnp.where((lane >= 16 * j - 8) & (lane < 16 * j), right, tile)
        flat_ref[:, cut] = tile.astype(BF)


def shift(flat, amount):
    return pltpu.roll(flat, amount % N, axis=1)


def rows_stack(dst, value, lane, sign):
    before = jnp.where(lane < PITCH, 0, shift(value, PITCH)).astype(BF)
    after = jnp.where(lane >= N - PITCH, 0, shift(value, -PITCH)).astype(BF)
    first, last = (before, after) if sign > 0 else (after, before)
    dst[0:C, :] = first
    dst[C : 2 * C, :] = value
    dst[2 * C : 3 * C, :] = last


def conv_pass(dst, weights, src):
    for start, size in CHUNKS:
        cut = slice(start, start + size)
        dst[:, cut] = mm(weights, src[:, cut])


def pack_share(dst, at, cg, eg, pg):
    blank = jnp.zeros((8, C), F32)
    for e in range(8):
        conv = [cg[c * C + 8 * e : c * C + 8 * e + 8, :] for c in range(3)]
        wide = [eg[32 * e + 8 * i : 32 * e + 8 * i + 8, :] for i in range(4)]
        tail = [conv[i][:, 128:192] for i in range(3)] + wide + [blank]
        units = [conv[i][:, 0:128] for i in range(3)]
        units += [pg[8 * e : 8 * e + 8, 0:128], pg[8 * e : 8 * e + 8, 128:256]]
        units += [jnp.concatenate(tail[2 * i : 2 * i + 2], axis=1) for i in range(4)]
        for i, unit in enumerate(units):
            dst[at, e, 8 * i : 8 * i + 8, :] = unit


def tile(ref, t, rows=slice(None)):
    return ref[rows, 128 * t : 128 * t + 128]


def span(t):
    return slice(128 * t, 128 * t + 128)


TILE_SETS = [[t for t in range(s // 128, (s + z) // 128)] for s, z in CHUNKS]
CUTS = [slice(s, s + z) for s, z in CHUNKS]
COUNT = len(CHUNKS)


def make_row_stack(src_ref, dst_ref, sign):
    lane = lax.broadcasted_iota(jnp.int32, (C, 128), 1)
    rolled = {}

    def roll16(t, way):
        if (t, way) not in rolled:
            rolled[t, way] = pltpu.roll(tile(src_ref, t), 16 * way % 128, axis=1)
        return rolled[t, way]

    def stack(t):
        if t < 2:
            before = jnp.zeros((C, 128), BF)
        elif t == 2:
            before = jnp.where(lane < 16, 0, roll16(0, 1)).astype(BF)
        else:
            before = jnp.where(lane < 16, roll16(t - 3, 1), roll16(t - 2, 1))
        if t > TILES - 3:
            after = jnp.zeros((C, 128), BF)
        elif t == TILES - 3:
            after = jnp.where(lane < 112, roll16(TILES - 1, -1), 0).astype(BF)
        else:
            after = jnp.where(lane < 112, roll16(t + 2, -1), roll16(t + 3, -1))
        first, last = (before, after) if sign > 0 else (after, before)
        dst_ref[0:C, span(t)] = first
        dst_ref[C : 2 * C, span(t)] = tile(src_ref, t)
        dst_ref[2 * C : 3 * C, span(t)] = last

    return stack


def make_neighbours(read_right, read_left):
    lane = lax.broadcasted_iota(jnp.int32, (C, 128), 1)
    right = {}
    left = {}

    def get(t):
        for k in (t - 1, t):
            if k not in right:
                right[k] = pltpu.roll(read_right(k % TILES), 1, axis=1)
        for k in (t, t + 1):
            if k not in left:
                left[k] = pltpu.roll(read_left(k % TILES), 127, axis=1)
        return jnp.where(lane < 1, right[t - 1], right[t]), jnp.where(lane < 127, left[t], left[t + 1])

    return get


def forward_stages(
    b, out_ref, stack_s, wide_s, hid_s, active_s, slope_s, conv_ref, expand_ref, bias_ref, project_ref
):
    stack = make_row_stack(out_ref, stack_s.at[b], 1)
    moved = make_neighbours(
        lambda t: tile(wide_s, t, slice(0, C)), lambda t: tile(wide_s, t, slice(2 * C, 3 * C))
    )

    def stacks(i):
        for t in TILE_SETS[i]:
            stack(t)

    def conv(i):
        wide_s[:, CUTS[i]] = mm(conv_ref[b], stack_s[b, :, CUTS[i]])

    def hidden(i):
        for t in TILE_SETS[i]:
            low, high = moved(t)
            hid_s[b, :, span(t)] = (low + tile(wide_s, t, slice(C, 2 * C)) + high).astype(BF)

    def expand(i):
        cut = CUTS[i]
        bias = jnp.concatenate([bias_ref[b]] * len(TILE_SETS[i]), axis=1)
        inner = mm(expand_ref[b], hid_s[b, :, cut]) + bias
        half = 0.5 + 0.5 * lax.erf(inner * SQRT_HALF)
        bell = jnp.exp2((inner * inner) * -HALF_LOG2E)
        slope_s[b, :, cut] = (half + (inner * INV_ROOT_TAU) * bell).astype(BF)
        active_s[b, :, cut] = (inner * half).astype(BF)

    def project(i):
        cut = CUTS[i]
        old = stack_s[b, C : 2 * C, cut].astype(F32)
        out_ref[:, cut] = (old + mm(project_ref[b], active_s[b, :, cut])).astype(BF)

    return [(stacks, 0), (conv, 1), (hidden, 2), (expand, 3), (project, 4)]


def backward_stages(
    b, up_ref, dh_ref, stack_s, rstack_s, own_s, wide_s, hid_s, active_s, slope_s, din_s, mask_s,
    convt_ref, expandt_ref, projectt_ref, sums,
):
    stack = make_row_stack(dh_ref, rstack_s, -1)
    moved = make_neighbours(
        lambda t: tile(wide_s, t, slice(2 * C, 3 * C)), lambda t: tile(wide_s, t, slice(0, C))
    )
    own_moved = make_neighbours(
        lambda t: tile(own_s, t, slice(C, 2 * C)), lambda t: tile(own_s, t, slice(C, 2 * C))
    )
    pg = []
    eg = []
    cg = []

    def inner(i):
        cut = CUTS[i]
        up = up_ref[:, cut]
        d_active = mm(projectt_ref[b], up)
        d_inner = (d_active * slope_s[b, :, cut].astype(F32)).astype(BF)
        din_s[:, cut] = d_inner
        pg.append(mm_nt(up * mask_s[:, cut], active_s[b, :, cut]))

    def hidden(i):
        cut = CUTS[i]
        d_inner = din_s[:, cut]
        d_hidden = mm(expandt_ref[b], d_inner).astype(BF)
        dh_ref[:, cut] = d_hidden
        own_s[C : 2 * C, cut] = d_hidden * mask_s[:, cut]
        eg.append(mm_nt(d_inner, hid_s[b, :, cut] * mask_s[:, cut]))

    def shares(i):
        for t in TILE_SETS[i]:
            right, left = own_moved(t)
            own_s[0:C, span(t)] = left
            own_s[2 * C : 3 * C, span(t)] = right
        cg.append(mm_nt(own_s[:, CUTS[i]], stack_s[b, :, CUTS[i]]))

    def stacks(i):
        for t in TILE_SETS[i]:
            stack(t)

    def conv(i):
        wide_s[:, CUTS[i]] = mm(convt_ref[b], rstack_s[:, CUTS[i]])

    def update(i):
        for t in TILE_SETS[i]:
            right, left = moved(t)
            total = tile(up_ref, t).astype(F32) + (left + tile(wide_s, t, slice(C, 2 * C)) + right)
            up_ref[:, span(t)] = total.astype(BF)

    def finish():
        sums[b] = (sum(cg[1:], cg[0]), sum(eg[1:], eg[0]), sum(pg[1:], pg[0]))

    stages = [(inner, 0), (hidden, 1), (shares, 3)]
    if b > 0:
        stages += [(stacks, 4), (conv, 5), (update, 7)]
    return stages, finish


def emit(jobs):
    last = max(first + max(lag for _, lag in stages) + COUNT for first, stages, _ in jobs)
    for step in range(last + 1):
        for first, stages, finish in jobs:
            for stage, lag in stages:
                i = step - first - lag
                if 0 <= i < COUNT:
                    stage(i)
            if finish is not None and step == first + max(lag for _, lag in stages) + COUNT:
                finish()


def main_kernel(
    field_ref,
    slope_ref,
    left_ref,
    right_ref,
    conv_ref,
    convt_ref,
    expand_ref,
    expandt_ref,
    bias_ref,
    project_ref,
    projectt_ref,
    out_ref,
    up_ref,
    dh_ref,
    own_ref,
    other_ref,
    stack_s,
    hid_s,
    active_s,
    slope_s,
    wide_s,
    rstack_s,
    share_s,
    own_s,
    din_s,
    mask_s,
):
    core = lax.axis_index("core")
    lane = lax.broadcasted_iota(jnp.int32, (C, N), 1)
    column = lane
    for row in range(1, H):
        column = jnp.where(lane >= row * PITCH, lane - row * PITCH, column)
    inside = (column >= HALO) & (column < HALO + WD)
    mask = jnp.where(inside, 1.0, 0.0).astype(BF)

    left = left_ref[...].astype(F32)
    right = right_ref[...].astype(F32)
    out_ref[...] = field_ref[...]
    add_halo(out_ref, left, pltpu.roll(right, 8, axis=1))
    up_ref[...] = slope_ref[...]
    add_halo(up_ref, pltpu.roll(left, 120, axis=1), right)

    mask_s[...] = mask
    wide_s[:, N - 128 : N] = jnp.zeros((3 * C, 128), F32)
    own_s[C : 2 * C, N - 128 : N] = jnp.zeros((C, 128), BF)
    jobs = []
    first = 0
    for b in range(DEPTH):
        stages = forward_stages(
            b, out_ref, stack_s, wide_s, hid_s, active_s, slope_s,
            conv_ref, expand_ref, bias_ref, project_ref,
        )
        jobs.append((first, stages, None))
        first += FORWARD_LAG
    first = first - FORWARD_LAG + TURN
    sums = {}

    def closing(b, finish):
        def run():
            finish()
            pack_share(share_s, b, *sums[b])

        return run

    for b in reversed(range(DEPTH)):
        stages, finish = backward_stages(
            b, up_ref, dh_ref, stack_s, rstack_s, own_s, wide_s, hid_s, active_s, slope_s, din_s,
            mask_s, convt_ref, expandt_ref, projectt_ref, sums,
        )
        jobs.append((first, stages, closing(b, finish)))
        first += BACKWARD_LAG
    emit(jobs)
    own_ref[...] = share_s[pl.ds(2 * core, 2)].reshape(16 * UNITS, 128).astype(BF)
    other_ref[...] = share_s[pl.ds(2 - 2 * core, 2)].reshape(16 * UNITS, 128).astype(BF)


def step_back(up_ref, dh_ref, weights, rstack_s, wide_s, lane):
    rows_stack(rstack_s, dh_ref[...], lane, -1)
    conv_pass(wide_s, weights, rstack_s)
    up_ref[...] = (
        up_ref[...].astype(F32)
        + (shift(wide_s[0:C, :], -1) + wide_s[C : 2 * C, :] + shift(wide_s[2 * C : 3 * C, :], 1))
    ).astype(BF)


def tail_kernel(
    orient_ref, flat_ref, up_in, dh_ref, convt_ref, out_ref, grad_ref, wide, up_s, rstack_s, wide_s
):
    flip = own_flip(orient_ref)
    lane = lax.broadcasted_iota(jnp.int32, (C, N), 1)
    up_s[...] = up_in[...]
    step_back(up_s, dh_ref, convt_ref[0], rstack_s, wide_s, lane)
    unflatten(flat_ref, out_ref, wide, flip)
    unflatten(up_s, grad_ref, wide, flip)


def unpack_kernel(src_ref, conv_ref, expand_ref, project_ref):
    for b in range(DEPTH):
        core, xl = b // 2, b % 2
        total = 0.0
        for y in range(4):
            total = total + src_ref[4 * y + 2 * xl + core].astype(F32)
        unit = [total[8 * i : 8 * i + 8, :] for i in range(9)]
        tail = []
        for i in range(5, 9):
            tail += [unit[i][:, 0:C], unit[i][:, C : 2 * C]]
        pieces = []
        for r in range(3):
            for c in range(3):
                pieces.append(tail[c] if r == 2 else unit[c][:, C * r : C * r + C])
        conv_ref[b] = jnp.concatenate(pieces, axis=1)
        for i in range(4):
            expand_ref[b, 8 * i : 8 * i + 8, :] = tail[3 + i]
        project_ref[b] = jnp.concatenate([unit[3], unit[4]], axis=1)


def main_scratch():
    return [
        pltpu.VMEM((DEPTH, 3 * C, N), BF),
        pltpu.VMEM((DEPTH, C, N), BF),
        pltpu.VMEM((DEPTH, HID, N), BF),
        pltpu.VMEM((DEPTH, HID, N), BF),
        pltpu.VMEM((3 * C, N), F32),
        pltpu.VMEM((3 * C, N), BF),
        pltpu.VMEM((DEPTH, 8, UNITS, 128), F32),
        pltpu.VMEM((3 * C, N), BF),
        pltpu.VMEM((HID, N), BF),
        pltpu.VMEM((C, N), BF),
    ]


def local(members_in, cotangent, conv_weight, expand_weight, expand_bias, project_weight, orient):
    field = members_in[0]
    slope = cotangent[0]
    wide = pltpu.VMEM((HALVES, C * H, 128), F32)
    low, high = call(
        edge_kernel,
        [shape(C, 128)] * 2,
        [(orient, True), (field, False), (slope, False)],
        [wide, wide],
        mib=12,
    )
    count = lax.axis_size(LON)
    left = lax.ppermute(high, LON, [(i, (i + 1) % count) for i in range(count)])
    right = lax.ppermute(low, LON, [((i + 1) % count, i) for i in range(count)])

    expandt = expand_weight.transpose(0, 2, 1)
    flat_f, flat_g, conv, convt, expand, projectt, bias = call(
        prep_kernel,
        [
            shape(C, N),
            shape(C, N),
            shape(DEPTH, 3 * C, 3 * C),
            shape(DEPTH, 3 * C, 3 * C),
            shape(DEPTH, HID, C),
            shape(DEPTH, HID, C),
            shape(DEPTH, HID, 128, dtype=F32),
        ],
        [
            (orient, True),
            (field, False),
            (slope, False),
            (conv_weight, False),
            (expandt, False),
            (expand_bias, False),
            (project_weight, False),
        ],
        [wide],
        flops=1 << 27,
        mib=16,
    )
    flat_out, up, d_hidden, own, other = call(
        main_kernel,
        [
            shape(C, N),
            shape(C, N),
            shape(C, N),
            shape(16 * UNITS, 128),
            shape(16 * UNITS, 128),
        ],
        [
            (flat_f, False),
            (flat_g, False),
            (left, False),
            (right, False),
            (conv, False),
            (convt, False),
            (expand, False),
            (expandt, False),
            (bias, False),
            (project_weight, False),
            (projectt, False),
        ],
        main_scratch(),
        flops=1 << 33,
        mib=40,
    )
    came = lax.ppermute(other, "core", [(0, 1), (1, 0)])
    share = (own.astype(F32) + came.astype(F32)).astype(BF)
    parts = lax.all_to_all(share.reshape(16, UNITS, 128), ("xl", "ens"), 0, 0, tiled=True)
    section_out, input_grad = call(
        tail_kernel,
        [shape(C, H, WD)] * 2,
        [(orient, True), (flat_out, False), (up, False), (d_hidden, False), (convt, False)],
        [wide, pltpu.VMEM((C, N), BF), pltpu.VMEM((3 * C, N), BF), pltpu.VMEM((3 * C, N), F32)],
        flops=1 << 30,
        mib=16,
    )
    total = jnp.sum(parts.astype(F32), axis=0).astype(BF)
    parts = jnp.broadcast_to(total[None], (count, UNITS, 128))
    parts = lax.all_to_all(parts, LON, 0, 0, tiled=True)
    conv_grad, expand_grad, project_grad = call(
        unpack_kernel,
        [
            shape(DEPTH, 8, 9 * C, dtype=F32),
            shape(DEPTH, 32, C, dtype=F32),
            shape(DEPTH, 8, HID, dtype=F32),
        ],
        [(parts, False)],
    )
    return section_out[None], input_grad[None], conv_grad, expand_grad, project_grad


def solution(mesh):
    split = Mesh(mesh.devices.reshape(4, 2, 2, 8), LON + ("ens",))
    cells = P("ens", None, None, LON)
    rows = P(None, "ens", None)
    return jax.shard_map(
        local,
        mesh=split,
        in_specs=(cells, cells, P(), P(), P(), P(), P()),
        out_specs=(cells, cells, rows, rows, rows),
        check_vma=False,
    )
```

```python
import jax
import jax.numpy as jnp
from jax import lax
from jax.experimental import pallas as pl
from jax.experimental.pallas import tpu as pltpu
from jax.sharding import Mesh
from jax.sharding import PartitionSpec as P

BF = jnp.bfloat16
VM = pltpu.VMEM
F32 = jnp.float32
SQRT_HALF = 0.7071067811865476
INV_ROOT_TAU = 0.3989422804014327
HALF_LOG2E = 0.7213475204444817

C = 64
HID = 256
H = 8
WD = 256
HALO = 8
PITCH = WD + 2 * HALO
N = H * PITCH
DEPTH = 4
HALVES = WD // 128
TILES = N // 128
UNITS = 72
BIAS_ROWS = 16
CHUNKS = [(s, min(256, N - s)) for s in range(0, N, 256)]
FORWARD_LAG = 8
BACKWARD_LAG = 8
TURN = 7


LON = ("y", "xl", "core")

NT = (((1,), (1,)), ((), ()))


def mm(a, b):
    return jnp.dot(a, b, preferred_element_type=F32)


def mm_nt(a, b):
    return lax.dot_general(a, b, NT, preferred_element_type=F32)


def call(body, outs, ins, scratch=(), flops=0, mib=8):
    specs = [pl.BlockSpec(memory_space=space) for _, space in ins]
    return pl.pallas_call(
        body,
        out_shape=outs,
        in_specs=specs,
        out_specs=jax.tree.map(lambda _: pl.BlockSpec(memory_space=pltpu.VMEM), outs),
        scratch_shapes=list(scratch),
        compiler_params=pltpu.CompilerParams(vmem_limit_bytes=mib << 20),
        cost_estimate=pl.CostEstimate(flops=flops, bytes_accessed=1 << 20, transcendentals=0),
    )(*[array for array, _ in ins])


def shape(*dims, dtype=BF):
    return jax.ShapeDtypeStruct(dims, dtype)


def spread(wide, ref):
    for half in range(HALVES):
        part = ref[:, :, 128 * half : 128 * half + 128]
        wide[half] = part.astype(F32).reshape(C * H, 128)


def stored_row(flip, row):
    return jnp.where(flip == 1, H - 1 - row, row)


def edge_kernel(*refs):
    orient_in, *sources = refs[0:7]
    low_ref, high_ref, flag_ref, *targets = refs[7:16]
    wide_f, wide_g, orient_s, sems = refs[16:20]
    copies = [pltpu.make_async_copy(orient_in, orient_s, sems.at[0])]
    for i, (source, target) in enumerate(zip(sources, targets)):
        copies.append(pltpu.make_async_copy(source, target, sems.at[i + 1]))
    for copy in copies:
        copy.start()
    for copy in copies[0:3]:
        copy.wait()
    sector = (lax.axis_index("y") * 2 + lax.axis_index("xl")) * 2 + lax.axis_index("core")
    flip = orient_s[sector]
    flag_ref[...] = jnp.full((8, 128), flip, jnp.int32)
    spread(wide_f, targets[0])
    spread(wide_g, targets[1])
    lane = lax.broadcasted_iota(jnp.int32, (C, 128), 1)
    low = jnp.zeros((C, 128), F32)
    high = jnp.zeros((C, 128), F32)
    for row in range(H):
        stored = stored_row(flip, row)
        for k, wide in ((0, wide_f), (8, wide_g)):
            at = 16 * row + k
            inside = (lane >= at) & (lane < at + 8)
            first = wide[0, pl.ds(stored, C, stride=H), :]
            last = wide[HALVES - 1, pl.ds(stored, C, stride=H), :]
            low = jnp.where(inside, pltpu.roll(first, at, axis=1), low)
            high = jnp.where(inside, pltpu.roll(last, (at + 8) % 128, axis=1), high)
    low_ref[...] = low.astype(BF)
    high_ref[...] = high.astype(BF)
    for copy in copies[3:]:
        copy.wait()


def flatten(ref, wide, flip):
    spread(wide, ref)
    edge = jnp.zeros((C, HALO), F32)
    parts = []
    for row in range(H):
        stored = stored_row(flip, row)
        parts.append(edge)
        for half in range(HALVES):
            parts.append(wide[half, pl.ds(stored, C, stride=H), :])
        parts.append(edge)
    return jnp.concatenate(parts, axis=1)


def unflatten(flat_ref, ref, wide, flip):
    for row in range(H):
        stored = stored_row(flip, row)
        for half in range(HALVES):
            at = row * PITCH + HALO + 128 * half
            wide[half, pl.ds(stored, C, stride=H), :] = flat_ref[:, at : at + 128].astype(F32)
    for half in range(HALVES):
        ref[:, :, 128 * half : 128 * half + 128] = wide[half].reshape(C, H, 128).astype(BF)


def prep_kernel(
    flag_ref,
    field_ref,
    slope_ref,
    kernel_ref,
    expandt_ref,
    bias_ref,
    project_ref,
    field_out,
    slope_out,
    conv_out,
    convt_out,
    expand_out,
    project_out,
    projectt_out,
    wide,
):
    flip = flag_ref[0, 0]
    field_out[...] = flatten(field_ref, wide, flip).astype(BF)
    slope_out[...] = flatten(slope_ref, wide, flip).astype(BF)
    lane = lax.broadcasted_iota(jnp.int32, (HID, 128), 1)
    for b in range(DEPTH):
        taps = kernel_ref[b]
        turned = taps.astype(F32).T
        for c in range(3):
            here = slice(c * C, c * C + C)
            at = [(3 * r + c) * C for r in range(3)]
            conv_out[b, here, :] = jnp.concatenate([taps[:, a : a + C] for a in at], axis=1)
            convt_out[b, here, :] = jnp.concatenate(
                [turned[a : a + C, :] for a in at], axis=1
            ).astype(BF)
        bias = jnp.broadcast_to(bias_ref[b : b + 1, :], (128, HID)).T
        high = bias.astype(BF).astype(F32)
        middle = (bias - high).astype(BF).astype(F32)
        low = bias - high - middle
        parts = jnp.where(lane == 0, high, jnp.where(lane == 1, middle, jnp.where(lane == 2, low, 0.0)))
        weight = jnp.concatenate([expandt_ref[b].astype(F32).T, parts[:, 0:BIAS_ROWS]], axis=1)
        expand_out[b] = weight.astype(BF)
        half = 0.5 * project_ref[b].astype(F32)
        project_out[b] = half.astype(BF)
        projectt_out[b] = half.T.astype(BF)


def add_halo(flat_ref, left, right):
    lane = lax.broadcasted_iota(jnp.int32, (C, 128), 1)
    for j in range(H + 1):
        cut = slice(256 * j, 256 * j + 128)
        tile = flat_ref[:, cut].astype(F32)
        tile = jnp.where((lane >= 16 * j) & (lane < 16 * j + 8), left, tile)
        tile = jnp.where((lane >= 16 * j - 8) & (lane < 16 * j), right, tile)
        flat_ref[:, cut] = tile.astype(BF)


def shift(flat, amount):
    return pltpu.roll(flat, amount % N, axis=1)


def rows_stack(dst, value, lane, sign):
    before = jnp.where(lane < PITCH, 0, shift(value, PITCH)).astype(BF)
    after = jnp.where(lane >= N - PITCH, 0, shift(value, -PITCH)).astype(BF)
    first, last = (before, after) if sign > 0 else (after, before)
    dst[0:C, :] = first
    dst[C : 2 * C, :] = value
    dst[2 * C : 3 * C, :] = last


def conv_pass(dst, weights, src):
    for start, size in CHUNKS:
        cut = slice(start, start + size)
        dst[:, cut] = mm(weights, src[:, cut])


def pack_share(dst, at, cg, eg, pg):
    blank = jnp.zeros((8, C), F32)
    for e in range(8):
        conv = [cg[c * C + 8 * e : c * C + 8 * e + 8, :] for c in range(3)]
        wide = [eg[32 * e + 8 * i : 32 * e + 8 * i + 8, :] for i in range(4)]
        tail = [conv[i][:, 128:192] for i in range(3)] + wide + [blank]
        units = [conv[i][:, 0:128] for i in range(3)]
        units += [pg[8 * e : 8 * e + 8, 0:128], pg[8 * e : 8 * e + 8, 128:256]]
        units += [jnp.concatenate(tail[2 * i : 2 * i + 2], axis=1) for i in range(4)]
        for i, unit in enumerate(units):
            dst[at, e, 8 * i : 8 * i + 8, :] = unit


def tile(ref, t, rows=slice(None)):
    return ref[rows, 128 * t : 128 * t + 128]


def span(t):
    return slice(128 * t, 128 * t + 128)


TILE_SETS = [[t for t in range(s // 128, (s + z) // 128)] for s, z in CHUNKS]
CUTS = [slice(s, s + z) for s, z in CHUNKS]
COUNT = len(CHUNKS)


def make_row_stack(src_ref, dst_ref, sign):
    lane = lax.broadcasted_iota(jnp.int32, (C, 128), 1)
    rolled = {}

    def roll16(t, way):
        if (t, way) not in rolled:
            rolled[t, way] = pltpu.roll(tile(src_ref, t), 16 * way % 128, axis=1)
        return rolled[t, way]

    def stack(t):
        if t < 2:
            before = jnp.zeros((C, 128), BF)
        elif t == 2:
            before = jnp.where(lane < 16, 0, roll16(0, 1)).astype(BF)
        else:
            before = jnp.where(lane < 16, roll16(t - 3, 1), roll16(t - 2, 1))
        if t > TILES - 3:
            after = jnp.zeros((C, 128), BF)
        elif t == TILES - 3:
            after = jnp.where(lane < 112, roll16(TILES - 1, -1), 0).astype(BF)
        else:
            after = jnp.where(lane < 112, roll16(t + 2, -1), roll16(t + 3, -1))
        first, last = (before, after) if sign > 0 else (after, before)
        dst_ref[0:C, span(t)] = first
        dst_ref[C : 2 * C, span(t)] = tile(src_ref, t)
        dst_ref[2 * C : 3 * C, span(t)] = last

    return stack


def make_neighbours(read_right, read_left):
    lane = lax.broadcasted_iota(jnp.int32, (C, 128), 1)
    right = {}
    left = {}

    def get(t):
        for k in (t - 1, t):
            if k not in right:
                right[k] = pltpu.roll(read_right(k % TILES), 1, axis=1)
        for k in (t, t + 1):
            if k not in left:
                left[k] = pltpu.roll(read_left(k % TILES), 127, axis=1)
        return jnp.where(lane < 1, right[t - 1], right[t]), jnp.where(lane < 127, left[t], left[t + 1])

    return get


def forward_stages(
    b, out_ref, stack_s, wide_s, hid_s, active_s, slope_s, conv_ref, expand_ref, project_ref, inner_s
):
    stack = make_row_stack(out_ref, stack_s.at[b], 1)
    moved = make_neighbours(
        lambda t: tile(wide_s, t, slice(0, C)), lambda t: tile(wide_s, t, slice(2 * C, 3 * C))
    )

    def stacks(i):
        for t in TILE_SETS[i]:
            stack(t)

    def conv(i):
        wide_s[:, CUTS[i]] = mm(conv_ref[b], stack_s[b, :, CUTS[i]])

    def hidden(i):
        for t in TILE_SETS[i]:
            low, high = moved(t)
            hid_s[b, 0:C, span(t)] = (low + tile(wide_s, t, slice(C, 2 * C)) + high).astype(BF)

    def expand(i):
        cut = CUTS[i]
        inner_s[:, cut] = mm(expand_ref[b], hid_s[b, :, cut])

    def gelu(i):
        cut = CUTS[i]
        inner = inner_s[:, cut]
        twice = 1.0 + lax.erf(inner * SQRT_HALF)
        bell = jnp.exp2((inner * inner) * -HALF_LOG2E)
        slope_s[b, :, cut] = (twice + (inner * (2.0 * INV_ROOT_TAU)) * bell).astype(BF)
        active_s[b, :, cut] = (inner * twice).astype(BF)

    def project(i):
        cut = CUTS[i]
        old = stack_s[b, C : 2 * C, cut].astype(F32)
        out_ref[:, cut] = (old + mm(project_ref[b], active_s[b, :, cut])).astype(BF)

    return [(gelu, 4), (hidden, 3), (stacks, 0), (conv, 1), (expand, 3), (project, 5)]


def backward_stages(
    b, up_ref, dh_ref, stack_s, rstack_s, own_s, wide_s, hid_s, active_s, slope_s, din_s, mask_s,
    convt_ref, expandt_ref, projectt_ref, sums,
):
    stack = make_row_stack(dh_ref, rstack_s, -1)
    moved = make_neighbours(
        lambda t: tile(wide_s, t, slice(2 * C, 3 * C)), lambda t: tile(wide_s, t, slice(0, C))
    )
    own_moved = make_neighbours(
        lambda t: tile(own_s, t, slice(C, 2 * C)), lambda t: tile(own_s, t, slice(C, 2 * C))
    )
    pg = []
    eg = []
    cg = []

    def inner(i):
        cut = CUTS[i]
        up = up_ref[:, cut]
        d_active = mm(projectt_ref[b], up)
        din_s[:, cut] = (d_active * slope_s[b, :, cut].astype(F32)).astype(BF)
        pg.append(mm_nt(up * mask_s[:, cut], active_s[b, :, cut]))

    def hidden(i):
        cut = CUTS[i]
        d_inner = din_s[:, cut]
        d_hidden = mm(expandt_ref[b], d_inner).astype(BF)
        dh_ref[:, cut] = d_hidden
        own_s[C : 2 * C, cut] = d_hidden * mask_s[:, cut]
        eg.append(mm_nt(d_inner, hid_s[b, 0:C, cut] * mask_s[:, cut]))

    def shares(i):
        for t in TILE_SETS[i]:
            right, left = own_moved(t)
            own_s[0:C, span(t)] = left
            own_s[2 * C : 3 * C, span(t)] = right
        cg.append(mm_nt(own_s[:, CUTS[i]], stack_s[b, :, CUTS[i]]))

    def stacks(i):
        for t in TILE_SETS[i]:
            stack(t)

    def conv(i):
        wide_s[:, CUTS[i]] = mm(convt_ref[b], rstack_s[:, CUTS[i]])

    def update(i):
        for t in TILE_SETS[i]:
            right, left = moved(t)
            total = tile(up_ref, t).astype(F32) + (left + tile(wide_s, t, slice(C, 2 * C)) + right)
            up_ref[:, span(t)] = total.astype(BF)

    def finish():
        sums[b] = (sum(cg[1:], cg[0]), sum(eg[1:], eg[0]), 0.5 * sum(pg[1:], pg[0]))

    stages = [(inner, 0), (hidden, 1), (shares, 3)]
    if b > 0:
        stages += [(stacks, 4), (conv, 5), (update, 7)]
    return stages, finish


def emit(jobs):
    last = max(first + max(lag for _, lag in stages) + COUNT for first, stages, _ in jobs)
    for step in range(last + 1):
        for first, stages, finish in jobs:
            for stage, lag in stages:
                i = step - first - lag
                if 0 <= i < COUNT:
                    stage(i)
            if finish is not None and step == first + max(lag for _, lag in stages) + COUNT:
                finish()


def main_kernel(
    field_ref,
    slope_ref,
    left_ref,
    right_ref,
    conv_ref,
    convt_ref,
    expand_ref,
    expandt_ref,
    project_ref,
    projectt_ref,
    out_ref,
    up_ref,
    dh_ref,
    own_ref,
    other_ref,
    stack_s,
    hid_s,
    active_s,
    slope_s,
    wide_s,
    rstack_s,
    share_s,
    own_s,
    din_s,
    mask_s,
    inner_s,
):
    core = lax.axis_index("core")
    lane = lax.broadcasted_iota(jnp.int32, (C, N), 1)
    column = lane
    for row in range(1, H):
        column = jnp.where(lane >= row * PITCH, lane - row * PITCH, column)
    inside = (column >= HALO) & (column < HALO + WD)
    mask = jnp.where(inside, 1.0, 0.0).astype(BF)

    left = left_ref[...].astype(F32)
    right = right_ref[...].astype(F32)
    out_ref[...] = field_ref[...]
    add_halo(out_ref, left, pltpu.roll(right, 8, axis=1))
    up_ref[...] = slope_ref[...]
    add_halo(up_ref, pltpu.roll(left, 120, axis=1), right)

    mask_s[...] = mask
    bias_row = lax.broadcasted_iota(jnp.int32, (BIAS_ROWS, N), 0)
    for b in range(DEPTH):
        hid_s[b, C : C + BIAS_ROWS, :] = jnp.where(bias_row < 3, 1.0, 0.0).astype(BF)
    wide_s[:, N - 128 : N] = jnp.zeros((3 * C, 128), F32)
    own_s[C : 2 * C, N - 128 : N] = jnp.zeros((C, 128), BF)
    jobs = []
    first = 0
    for b in range(DEPTH):
        stages = forward_stages(
            b, out_ref, stack_s, wide_s, hid_s, active_s, slope_s,
            conv_ref, expand_ref, project_ref, inner_s,
        )
        jobs.append((first, stages, None))
        first += FORWARD_LAG
    first = first - FORWARD_LAG + TURN
    sums = {}

    def closing(b, finish):
        def run():
            finish()
            pack_share(share_s, b, *sums[b])

        return run

    for b in reversed(range(DEPTH)):
        stages, finish = backward_stages(
            b, up_ref, dh_ref, stack_s, rstack_s, own_s, wide_s, hid_s, active_s, slope_s, din_s,
            mask_s, convt_ref, expandt_ref, projectt_ref, sums,
        )
        jobs.append((first, stages, closing(b, finish)))
        first += BACKWARD_LAG
    emit(jobs)
    own_ref[...] = share_s[pl.ds(2 * core, 2)].reshape(16 * UNITS, 128).astype(BF)
    other_ref[...] = share_s[pl.ds(2 - 2 * core, 2)].reshape(16 * UNITS, 128).astype(BF)


def step_back(up_ref, dh_ref, weights, rstack_s, wide_s, lane):
    rows_stack(rstack_s, dh_ref[...], lane, -1)
    conv_pass(wide_s, weights, rstack_s)
    up_ref[...] = (
        up_ref[...].astype(F32)
        + (shift(wide_s[0:C, :], -1) + wide_s[C : 2 * C, :] + shift(wide_s[2 * C : 3 * C, :], 1))
    ).astype(BF)


def tail_kernel(
    flag_ref, flat_ref, up_in, dh_ref, convt_ref, out_ref, grad_ref, wide, up_s, rstack_s, wide_s
):
    flip = flag_ref[0, 0]
    lane = lax.broadcasted_iota(jnp.int32, (C, N), 1)
    up_s[...] = up_in[...]
    step_back(up_s, dh_ref, convt_ref[0], rstack_s, wide_s, lane)
    unflatten(flat_ref, out_ref, wide, flip)
    unflatten(up_s, grad_ref, wide, flip)


def unpack_kernel(src_ref, conv_ref, expand_ref, project_ref):
    for b in range(DEPTH):
        core, xl = b // 2, b % 2
        total = 0.0
        for y in range(4):
            total = total + src_ref[4 * y + 2 * xl + core].astype(F32)
        unit = [total[8 * i : 8 * i + 8, :] for i in range(9)]
        tail = []
        for i in range(5, 9):
            tail += [unit[i][:, 0:C], unit[i][:, C : 2 * C]]
        pieces = []
        for r in range(3):
            for c in range(3):
                pieces.append(tail[c] if r == 2 else unit[c][:, C * r : C * r + C])
        conv_ref[b] = jnp.concatenate(pieces, axis=1)
        for i in range(4):
            expand_ref[b, 8 * i : 8 * i + 8, :] = tail[3 + i]
        project_ref[b] = jnp.concatenate([unit[3], unit[4]], axis=1)


def main_scratch():
    return [
        pltpu.VMEM((DEPTH, 3 * C, N), BF),
        pltpu.VMEM((DEPTH, C + BIAS_ROWS, N), BF),
        pltpu.VMEM((DEPTH, HID, N), BF),
        pltpu.VMEM((DEPTH, HID, N), BF),
        pltpu.VMEM((3 * C, N), F32),
        pltpu.VMEM((3 * C, N), BF),
        pltpu.VMEM((DEPTH, 8, UNITS, 128), F32),
        pltpu.VMEM((3 * C, N), BF),
        pltpu.VMEM((HID, N), BF),
        pltpu.VMEM((C, N), BF),
        pltpu.VMEM((HID, N), F32),
    ]


def local(members_in, cotangent, conv_weight, expand_weight, expand_bias, project_weight, orient):
    field = members_in[0]
    slope = cotangent[0]
    wide = pltpu.VMEM((HALVES, C * H, 128), F32)
    sources = [field, slope, conv_weight, expand_weight.transpose(0, 2, 1), expand_bias, project_weight]
    low, high, flag, field, slope, taps, expandt, bias, weight = call(
        edge_kernel,
        [shape(C, 128), shape(C, 128), shape(8, 128, dtype=jnp.int32)]
        + [shape(*array.shape, dtype=array.dtype) for array in sources],
        [(pltpu.with_memory_space_constraint(array, pltpu.HBM), pl.ANY) for array in [orient] + sources],
        [wide, wide, pltpu.SMEM((16,), jnp.int32), pltpu.SemaphoreType.DMA((7,))],
        mib=8,
    )
    count = lax.axis_size(LON)
    left = lax.ppermute(high, LON, [(i, (i + 1) % count) for i in range(count)])
    right = lax.ppermute(low, LON, [((i + 1) % count, i) for i in range(count)])

    flat_f, flat_g, conv, convt, expand, project, projectt = call(
        prep_kernel,
        [
            shape(C, N),
            shape(C, N),
            shape(DEPTH, 3 * C, 3 * C),
            shape(DEPTH, 3 * C, 3 * C),
            shape(DEPTH, HID, C + BIAS_ROWS),
            shape(DEPTH, C, HID),
            shape(DEPTH, HID, C),
        ],
        [
            (flag, VM),
            (field, VM),
            (slope, VM),
            (taps, VM),
            (expandt, VM),
            (bias, VM),
            (weight, VM),
        ],
        [wide],
        flops=1 << 27,
        mib=16,
    )
    flat_out, up, d_hidden, own, other = call(
        main_kernel,
        [
            shape(C, N),
            shape(C, N),
            shape(C, N),
            shape(16 * UNITS, 128),
            shape(16 * UNITS, 128),
        ],
        [
            (flat_f, VM),
            (flat_g, VM),
            (left, VM),
            (right, VM),
            (conv, VM),
            (convt, VM),
            (expand, VM),
            (expandt, VM),
            (project, VM),
            (projectt, VM),
        ],
        main_scratch(),
        flops=1 << 33,
        mib=40,
    )
    came = lax.ppermute(other, "core", [(0, 1), (1, 0)])
    share = (own.astype(F32) + came.astype(F32)).astype(BF)
    parts = lax.all_to_all(share.reshape(16, UNITS, 128), ("xl", "ens"), 0, 0, tiled=True)
    section_out, input_grad = call(
        tail_kernel,
        [shape(C, H, WD)] * 2,
        [(flag, VM), (flat_out, VM), (up, VM), (d_hidden, VM), (convt, VM)],
        [wide, pltpu.VMEM((C, N), BF), pltpu.VMEM((3 * C, N), BF), pltpu.VMEM((3 * C, N), F32)],
        flops=1 << 30,
        mib=16,
    )
    total = jnp.sum(parts.astype(F32), axis=0).astype(BF)
    parts = jnp.broadcast_to(total[None], (count, UNITS, 128))
    parts = lax.all_to_all(parts, LON, 0, 0, tiled=True)
    conv_grad, expand_grad, project_grad = call(
        unpack_kernel,
        [
            shape(DEPTH, 8, 9 * C, dtype=F32),
            shape(DEPTH, 32, C, dtype=F32),
            shape(DEPTH, 8, HID, dtype=F32),
        ],
        [(parts, VM)],
    )
    return section_out[None], input_grad[None], conv_grad, expand_grad, project_grad


def solution(mesh):
    split = Mesh(mesh.devices.reshape(4, 2, 2, 8), LON + ("ens",))
    cells = P("ens", None, None, LON)
    rows = P(None, "ens", None)
    return jax.shard_map(
        local,
        mesh=split,
        in_specs=(cells, cells, P(), P(), P(), P(), P()),
        out_specs=(cells, cells, rows, rows, rows),
        check_vma=False,
    )
```

```python
import jax
import jax.numpy as jnp
from jax import lax
from jax.experimental import pallas as pl
from jax.experimental.pallas import tpu as pltpu
from jax.sharding import Mesh
from jax.sharding import PartitionSpec as P

BF = jnp.bfloat16
VM = pltpu.VMEM
F32 = jnp.float32
SQRT_HALF = 0.7071067811865476
INV_ROOT_TAU = 0.3989422804014327
HALF_LOG2E = 0.7213475204444817

C = 64
HID = 256
H = 8
WD = 256
HALO = 8
PITCH = WD + 2 * HALO
N = H * PITCH
DEPTH = 4
HALVES = WD // 128
TILES = N // 128
UNITS = 72
BIAS_ROWS = 16
CHUNKS = [(s, min(256, N - s)) for s in range(0, N, 256)]
FORWARD_LAG = 9
BACKWARD_LAG = 8
TURN = 8


LON = ("y", "xl", "core")

NT = (((1,), (1,)), ((), ()))


def mm(a, b):
    return jnp.dot(a, b, preferred_element_type=F32)


def mm_nt(a, b):
    return lax.dot_general(a, b, NT, preferred_element_type=F32)


def call(body, outs, ins, scratch=(), flops=0, mib=8):
    specs = [pl.BlockSpec(memory_space=space) for _, space in ins]
    return pl.pallas_call(
        body,
        out_shape=outs,
        in_specs=specs,
        out_specs=jax.tree.map(lambda _: pl.BlockSpec(memory_space=pltpu.VMEM), outs),
        scratch_shapes=list(scratch),
        compiler_params=pltpu.CompilerParams(vmem_limit_bytes=mib << 20),
        cost_estimate=pl.CostEstimate(flops=flops, bytes_accessed=1 << 20, transcendentals=0),
    )(*[array for array, _ in ins])


def shape(*dims, dtype=BF):
    return jax.ShapeDtypeStruct(dims, dtype)


def spread(wide, ref):
    for half in range(HALVES):
        part = ref[:, :, 128 * half : 128 * half + 128]
        wide[half] = part.astype(F32).reshape(C * H, 128)


def stored_row(flip, row):
    return jnp.where(flip == 1, H - 1 - row, row)


def edge_kernel(*refs):
    orient_in, *sources = refs[0:7]
    inner_ref, outer_ref, flag_ref, *targets = refs[7:16]
    wide_f, wide_g, orient_s, sems = refs[16:20]
    copies = [pltpu.make_async_copy(orient_in, orient_s, sems.at[0])]
    for i, (source, target) in enumerate(zip(sources, targets)):
        copies.append(pltpu.make_async_copy(source, target, sems.at[i + 1]))
    for copy in copies:
        copy.start()
    for copy in copies[0:3]:
        copy.wait()
    sector = (lax.axis_index("y") * 2 + lax.axis_index("xl")) * 2 + lax.axis_index("core")
    flip = orient_s[sector]
    flag_ref[...] = jnp.full((8, 128), flip, jnp.int32)
    spread(wide_f, targets[0])
    spread(wide_g, targets[1])
    lane = lax.broadcasted_iota(jnp.int32, (C, 128), 1)
    low = jnp.zeros((C, 128), F32)
    high = jnp.zeros((C, 128), F32)
    for row in range(H):
        stored = stored_row(flip, row)
        for k, wide in ((0, wide_f), (8, wide_g)):
            at = 16 * row + k
            inside = (lane >= at) & (lane < at + 8)
            first = wide[0, pl.ds(stored, C, stride=H), :]
            last = wide[HALVES - 1, pl.ds(stored, C, stride=H), :]
            low = jnp.where(inside, pltpu.roll(first, at, axis=1), low)
            high = jnp.where(inside, pltpu.roll(last, (at + 8) % 128, axis=1), high)
    first = lax.axis_index("core") == 0
    inner_ref[...] = jnp.where(first, high, low).astype(BF)
    outer_ref[...] = jnp.where(first, low, high).astype(BF)
    for copy in copies[3:]:
        copy.wait()


def flatten(ref, wide, flip):
    spread(wide, ref)
    edge = jnp.zeros((C, HALO), F32)
    parts = []
    for row in range(H):
        stored = stored_row(flip, row)
        parts.append(edge)
        for half in range(HALVES):
            parts.append(wide[half, pl.ds(stored, C, stride=H), :])
        parts.append(edge)
    return jnp.concatenate(parts, axis=1)


def unflatten(flat_ref, ref, wide, flip):
    for row in range(H):
        stored = stored_row(flip, row)
        for half in range(HALVES):
            at = row * PITCH + HALO + 128 * half
            wide[half, pl.ds(stored, C, stride=H), :] = flat_ref[:, at : at + 128].astype(F32)
    for half in range(HALVES):
        ref[:, :, 128 * half : 128 * half + 128] = wide[half].reshape(C, H, 128).astype(BF)


def prep_kernel(
    flag_ref,
    field_ref,
    slope_ref,
    kernel_ref,
    expandt_ref,
    bias_ref,
    project_ref,
    field_out,
    slope_out,
    conv_out,
    convt_out,
    expand_out,
    project_out,
    projectt_out,
    mask_out,
    wide,
):
    flip = flag_ref[0, 0]
    field_out[...] = flatten(field_ref, wide, flip).astype(BF)
    slope_out[...] = flatten(slope_ref, wide, flip).astype(BF)
    lane = lax.broadcasted_iota(jnp.int32, (16, N), 1)
    column = lane
    for row in range(1, H):
        column = jnp.where(lane >= row * PITCH, lane - row * PITCH, column)
    mask = jnp.where((column >= HALO) & (column < HALO + WD), 1.0, 0.0).astype(BF)
    for k in range(0, C, 16):
        mask_out[k : k + 16, :] = mask
    lane = lax.broadcasted_iota(jnp.int32, (HID, 128), 1)
    for b in range(DEPTH):
        taps = kernel_ref[b]
        turned = taps.astype(F32).T
        for c in range(3):
            here = slice(c * C, c * C + C)
            at = [(3 * r + c) * C for r in range(3)]
            conv_out[b, here, :] = jnp.concatenate([taps[:, a : a + C] for a in at], axis=1)
            convt_out[b, here, :] = jnp.concatenate(
                [turned[a : a + C, :] for a in at], axis=1
            ).astype(BF)
        bias = jnp.broadcast_to(bias_ref[b : b + 1, :], (128, HID)).T
        high = bias.astype(BF).astype(F32)
        middle = (bias - high).astype(BF).astype(F32)
        low = bias - high - middle
        parts = jnp.where(lane == 0, high, jnp.where(lane == 1, middle, jnp.where(lane == 2, low, 0.0)))
        weight = jnp.concatenate([expandt_ref[b].astype(F32).T, parts[:, 0:BIAS_ROWS]], axis=1)
        expand_out[b] = weight.astype(BF)
        half = 0.5 * project_ref[b].astype(F32)
        project_out[b] = half.astype(BF)
        projectt_out[b] = half.T.astype(BF)


def add_halo(flat_ref, left, right):
    lane = lax.broadcasted_iota(jnp.int32, (C, 128), 1)
    for j in range(H + 1):
        cut = slice(256 * j, 256 * j + 128)
        tile = flat_ref[:, cut].astype(F32)
        tile = jnp.where((lane >= 16 * j) & (lane < 16 * j + 8), left, tile)
        tile = jnp.where((lane >= 16 * j - 8) & (lane < 16 * j), right, tile)
        flat_ref[:, cut] = tile.astype(BF)


def shift(flat, amount):
    return pltpu.roll(flat, amount % N, axis=1)


def rows_stack(dst, value, lane, sign):
    before = jnp.where(lane < PITCH, 0, shift(value, PITCH)).astype(BF)
    after = jnp.where(lane >= N - PITCH, 0, shift(value, -PITCH)).astype(BF)
    first, last = (before, after) if sign > 0 else (after, before)
    dst[0:C, :] = first
    dst[C : 2 * C, :] = value
    dst[2 * C : 3 * C, :] = last


def conv_pass(dst, weights, src):
    for start, size in CHUNKS:
        cut = slice(start, start + size)
        dst[:, cut] = mm(weights, src[:, cut])


def pack_share(dst, at, cg, eg, pg):
    blank = jnp.zeros((8, C), F32)
    for e in range(8):
        conv = [cg[c * C + 8 * e : c * C + 8 * e + 8, :] for c in range(3)]
        wide = [eg[32 * e + 8 * i : 32 * e + 8 * i + 8, :] for i in range(4)]
        tail = [conv[i][:, 128:192] for i in range(3)] + wide + [blank]
        units = [conv[i][:, 0:128] for i in range(3)]
        units += [pg[8 * e : 8 * e + 8, 0:128], pg[8 * e : 8 * e + 8, 128:256]]
        units += [jnp.concatenate(tail[2 * i : 2 * i + 2], axis=1) for i in range(4)]
        for i, unit in enumerate(units):
            dst[at, e, 8 * i : 8 * i + 8, :] = unit


def tile(ref, t, rows=slice(None)):
    return ref[rows, 128 * t : 128 * t + 128]


def span(t):
    return slice(128 * t, 128 * t + 128)


TILE_SETS = [[t for t in range(s // 128, (s + z) // 128)] for s, z in CHUNKS]
CUTS = [slice(s, s + z) for s, z in CHUNKS]
COUNT = len(CHUNKS)


def make_row_stack(src_ref, dst_ref, sign):
    lane = lax.broadcasted_iota(jnp.int32, (C, 128), 1)
    rolled = {}

    def roll16(t, way):
        if (t, way) not in rolled:
            rolled[t, way] = pltpu.roll(tile(src_ref, t), 16 * way % 128, axis=1)
        return rolled[t, way]

    def stack(t):
        if t < 2:
            before = jnp.zeros((C, 128), BF)
        elif t == 2:
            before = jnp.where(lane < 16, 0, roll16(0, 1)).astype(BF)
        else:
            before = jnp.where(lane < 16, roll16(t - 3, 1), roll16(t - 2, 1))
        if t > TILES - 3:
            after = jnp.zeros((C, 128), BF)
        elif t == TILES - 3:
            after = jnp.where(lane < 112, roll16(TILES - 1, -1), 0).astype(BF)
        else:
            after = jnp.where(lane < 112, roll16(t + 2, -1), roll16(t + 3, -1))
        first, last = (before, after) if sign > 0 else (after, before)
        dst_ref[0:C, span(t)] = first
        dst_ref[C : 2 * C, span(t)] = tile(src_ref, t)
        dst_ref[2 * C : 3 * C, span(t)] = last

    return stack


def make_neighbours(read_right, read_left):
    lane = lax.broadcasted_iota(jnp.int32, (C, 128), 1)
    right = {}
    left = {}

    def get(t):
        for k in (t - 1, t):
            if k not in right:
                right[k] = pltpu.roll(read_right(k % TILES), 1, axis=1)
        for k in (t, t + 1):
            if k not in left:
                left[k] = pltpu.roll(read_left(k % TILES), 127, axis=1)
        return jnp.where(lane < 1, right[t - 1], right[t]), jnp.where(lane < 127, left[t], left[t + 1])

    return get


def forward_stages(
    b, out_ref, stack_s, wide_s, hid_s, active_s, slope_s, conv_ref, expand_ref, project_ref, inner_s
):
    stack = make_row_stack(out_ref, stack_s.at[b], 1)
    moved = make_neighbours(
        lambda t: tile(wide_s, t, slice(0, C)), lambda t: tile(wide_s, t, slice(2 * C, 3 * C))
    )

    def stacks(i):
        for t in TILE_SETS[i]:
            stack(t)

    def conv(i):
        wide_s[:, CUTS[i]] = mm(conv_ref[b], stack_s[b, :, CUTS[i]])

    def hidden(i):
        for t in TILE_SETS[i]:
            low, high = moved(t)
            hid_s[b, 0:C, span(t)] = (low + tile(wide_s, t, slice(C, 2 * C)) + high).astype(BF)

    def expand(i):
        cut = CUTS[i]
        inner_s[:, cut] = mm(expand_ref[b], hid_s[b, :, cut])

    def gelu(i):
        cut = CUTS[i]
        inner = inner_s[:, cut]
        twice = 1.0 + lax.erf(inner * SQRT_HALF)
        bell = jnp.exp2((inner * inner) * -HALF_LOG2E)
        slope_s[b, :, cut] = (twice + (inner * (2.0 * INV_ROOT_TAU)) * bell).astype(BF)
        active_s[b, :, cut] = (inner * twice).astype(BF)

    def project(i):
        cut = CUTS[i]
        old = stack_s[b, C : 2 * C, cut].astype(F32)
        out_ref[:, cut] = (old + mm(project_ref[b], active_s[b, :, cut])).astype(BF)

    return [(conv, 1), (gelu, 5), (expand, 4), (hidden, 3), (project, 6), (stacks, 0)]


def backward_stages(
    b, up_ref, dh_ref, stack_s, rstack_s, own_s, wide_s, hid_s, active_s, slope_s, din_s, mask_s,
    convt_ref, expandt_ref, projectt_ref, sums,
):
    stack = make_row_stack(dh_ref, rstack_s, -1)
    moved = make_neighbours(
        lambda t: tile(wide_s, t, slice(2 * C, 3 * C)), lambda t: tile(wide_s, t, slice(0, C))
    )
    own_moved = make_neighbours(
        lambda t: tile(own_s, t, slice(C, 2 * C)), lambda t: tile(own_s, t, slice(C, 2 * C))
    )
    pg = []
    eg = []
    cg = []

    def inner(i):
        cut = CUTS[i]
        up = up_ref[:, cut]
        d_active = mm(projectt_ref[b], up)
        din_s[:, cut] = (d_active * slope_s[b, :, cut].astype(F32)).astype(BF)
        pg.append(mm_nt(up * mask_s[:, cut], active_s[b, :, cut]))

    def hidden(i):
        cut = CUTS[i]
        d_inner = din_s[:, cut]
        d_hidden = mm(expandt_ref[b], d_inner).astype(BF)
        dh_ref[:, cut] = d_hidden
        own_s[C : 2 * C, cut] = d_hidden * mask_s[:, cut]
        eg.append(mm_nt(d_inner, hid_s[b, 0:C, cut] * mask_s[:, cut]))

    def shares(i):
        for t in TILE_SETS[i]:
            right, left = own_moved(t)
            own_s[0:C, span(t)] = left
            own_s[2 * C : 3 * C, span(t)] = right
        cg.append(mm_nt(own_s[:, CUTS[i]], stack_s[b, :, CUTS[i]]))

    def stacks(i):
        for t in TILE_SETS[i]:
            stack(t)

    def conv(i):
        wide_s[:, CUTS[i]] = mm(convt_ref[b], rstack_s[:, CUTS[i]])

    def update(i):
        for t in TILE_SETS[i]:
            right, left = moved(t)
            total = tile(up_ref, t).astype(F32) + (left + tile(wide_s, t, slice(C, 2 * C)) + right)
            up_ref[:, span(t)] = total.astype(BF)

    def finish():
        sums[b] = (sum(cg[1:], cg[0]), sum(eg[1:], eg[0]), 0.5 * sum(pg[1:], pg[0]))

    stages = [(inner, 0), (hidden, 1), (shares, 3)]
    if b > 0:
        stages += [(stacks, 4), (conv, 5), (update, 7)]
    return stages, finish


def emit(jobs):
    last = max(first + max(lag for _, lag in stages) + COUNT for first, stages, _ in jobs)
    for step in range(last + 1):
        for first, stages, finish in jobs:
            for stage, lag in stages:
                i = step - first - lag
                if 0 <= i < COUNT:
                    stage(i)
            if finish is not None and step == first + max(lag for _, lag in stages) + COUNT:
                finish()


def main_kernel(
    field_ref,
    slope_ref,
    inner_ref,
    outer_ref,
    conv_ref,
    convt_ref,
    expand_ref,
    expandt_ref,
    project_ref,
    projectt_ref,
    mask_s,
    out_ref,
    up_ref,
    dh_ref,
    own_ref,
    other_ref,
    stack_s,
    hid_s,
    active_s,
    slope_s,
    wide_s,
    rstack_s,
    share_s,
    own_s,
    din_s,
    inner_s,
):
    core = lax.axis_index("core")
    first = core == 0
    inner = inner_ref[...].astype(F32)
    outer = outer_ref[...].astype(F32)
    left = jnp.where(first, outer, inner)
    right = jnp.where(first, inner, outer)
    out_ref[...] = field_ref[...]
    add_halo(out_ref, left, pltpu.roll(right, 8, axis=1))
    up_ref[...] = slope_ref[...]
    add_halo(up_ref, pltpu.roll(left, 120, axis=1), right)

    bias_row = lax.broadcasted_iota(jnp.int32, (BIAS_ROWS, N), 0)
    for b in range(DEPTH):
        hid_s[b, C : C + BIAS_ROWS, :] = jnp.where(bias_row < 3, 1.0, 0.0).astype(BF)
    wide_s[:, N - 128 : N] = jnp.zeros((3 * C, 128), F32)
    own_s[C : 2 * C, N - 128 : N] = jnp.zeros((C, 128), BF)
    jobs = []
    first = 0
    for b in range(DEPTH):
        stages = forward_stages(
            b, out_ref, stack_s, wide_s, hid_s, active_s, slope_s,
            conv_ref, expand_ref, project_ref, inner_s,
        )
        jobs.append((first, stages, None))
        first += FORWARD_LAG
    first = first - FORWARD_LAG + TURN
    sums = {}

    def closing(b, finish):
        def run():
            finish()
            pack_share(share_s, b, *sums[b])

        return run

    for b in reversed(range(DEPTH)):
        stages, finish = backward_stages(
            b, up_ref, dh_ref, stack_s, rstack_s, own_s, wide_s, hid_s, active_s, slope_s, din_s,
            mask_s, convt_ref, expandt_ref, projectt_ref, sums,
        )
        jobs.append((first, stages, closing(b, finish)))
        first += BACKWARD_LAG
    emit(jobs)
    own_ref[...] = share_s[pl.ds(2 * core, 2)].reshape(16 * UNITS, 128).astype(BF)
    other_ref[...] = share_s[pl.ds(2 - 2 * core, 2)].reshape(16 * UNITS, 128).astype(BF)


def step_back(up_ref, dh_ref, weights, rstack_s, wide_s, lane):
    rows_stack(rstack_s, dh_ref[...], lane, -1)
    conv_pass(wide_s, weights, rstack_s)
    up_ref[...] = (
        up_ref[...].astype(F32)
        + (shift(wide_s[0:C, :], -1) + wide_s[C : 2 * C, :] + shift(wide_s[2 * C : 3 * C, :], 1))
    ).astype(BF)


def tail_kernel(
    flag_ref, flat_ref, up_in, dh_ref, convt_ref, out_ref, grad_ref, blank_ref, wide, up_s, rstack_s, wide_s
):
    flip = flag_ref[0, 0]
    lane = lax.broadcasted_iota(jnp.int32, (C, N), 1)
    up_s[...] = up_in[...]
    step_back(up_s, dh_ref, convt_ref[0], rstack_s, wide_s, lane)
    blank_ref[...] = jnp.zeros((UNITS, 128), F32)
    unflatten(flat_ref, out_ref, wide, flip)
    unflatten(up_s, grad_ref, wide, flip)


def unpack_kernel(mine_ref, theirs_ref, conv_ref, expand_ref, project_ref):
    core = lax.axis_index("core")
    for source, pair in ((mine_ref, core), (theirs_ref, 1 - core)):
        for xl in range(2):
            unpack_block(source[xl].astype(F32), 2 * pair + xl, conv_ref, expand_ref, project_ref)


def unpack_block(total, b, conv_ref, expand_ref, project_ref):
    unit = [total[8 * i : 8 * i + 8, :] for i in range(9)]
    tail = []
    for i in range(5, 9):
        tail += [unit[i][:, 0:C], unit[i][:, C : 2 * C]]
    pieces = []
    for r in range(3):
        for c in range(3):
            pieces.append(tail[c] if r == 2 else unit[c][:, C * r : C * r + C])
    conv_ref[b] = jnp.concatenate(pieces, axis=1)
    for i in range(4):
        expand_ref[b, 8 * i : 8 * i + 8, :] = tail[3 + i]
    project_ref[b] = jnp.concatenate([unit[3], unit[4]], axis=1)


def main_scratch():
    return [
        pltpu.VMEM((DEPTH, 3 * C, N), BF),
        pltpu.VMEM((DEPTH, C + BIAS_ROWS, N), BF),
        pltpu.VMEM((DEPTH, HID, N), BF),
        pltpu.VMEM((DEPTH, HID, N), BF),
        pltpu.VMEM((3 * C, N), F32),
        pltpu.VMEM((3 * C, N), BF),
        pltpu.VMEM((DEPTH, 8, UNITS, 128), F32),
        pltpu.VMEM((3 * C, N), BF),
        pltpu.VMEM((HID, N), BF),
        pltpu.VMEM((HID, N), F32),
    ]


def local(members_in, cotangent, conv_weight, expand_weight, expand_bias, project_weight, orient):
    field = members_in[0]
    slope = cotangent[0]
    wide = pltpu.VMEM((HALVES, C * H, 128), F32)
    sources = [field, slope, conv_weight, expand_weight.transpose(0, 2, 1), expand_bias, project_weight]
    inner, outer, flag, field, slope, taps, expandt, bias, weight = call(
        edge_kernel,
        [shape(C, 128), shape(C, 128), shape(8, 128, dtype=jnp.int32)]
        + [shape(*array.shape, dtype=array.dtype) for array in sources],
        [(pltpu.with_memory_space_constraint(array, pltpu.HBM), pl.ANY) for array in [orient] + sources],
        [wide, wide, pltpu.SMEM((16,), jnp.int32), pltpu.SemaphoreType.DMA((7,))],
        mib=8,
    )
    count = lax.axis_size(LON)
    inner = lax.ppermute(inner, "core", [(0, 1), (1, 0)])
    across = [(i, (i + 1) % count) for i in range(1, count, 2)]
    outer = lax.ppermute(outer, LON, across + [(target, source) for source, target in across])

    flat_f, flat_g, conv, convt, expand, project, projectt, mask = call(
        prep_kernel,
        [
            shape(C, N),
            shape(C, N),
            shape(DEPTH, 3 * C, 3 * C),
            shape(DEPTH, 3 * C, 3 * C),
            shape(DEPTH, HID, C + BIAS_ROWS),
            shape(DEPTH, C, HID),
            shape(DEPTH, HID, C),
            shape(C, N),
        ],
        [
            (flag, VM),
            (field, VM),
            (slope, VM),
            (taps, VM),
            (expandt, VM),
            (bias, VM),
            (weight, VM),
        ],
        [wide],
        flops=1 << 27,
        mib=16,
    )
    flat_out, up, d_hidden, own, other = call(
        main_kernel,
        [
            shape(C, N),
            shape(C, N),
            shape(C, N),
            shape(16 * UNITS, 128),
            shape(16 * UNITS, 128),
        ],
        [
            (flat_f, VM),
            (flat_g, VM),
            (inner, VM),
            (outer, VM),
            (conv, VM),
            (convt, VM),
            (expand, VM),
            (expandt, VM),
            (project, VM),
            (projectt, VM),
            (mask, VM),
        ],
        main_scratch(),
        flops=1 << 33,
        mib=40,
    )
    came = lax.ppermute(other, "core", [(0, 1), (1, 0)])
    share = (own.astype(F32) + came.astype(F32)).astype(BF)
    parts = lax.all_to_all(share.reshape(16, UNITS, 128), ("xl", "ens"), 0, 0, tiled=True)
    section_out, input_grad, blank = call(
        tail_kernel,
        [shape(C, H, WD)] * 2 + [shape(UNITS, 128, dtype=F32)],
        [(flag, VM), (flat_out, VM), (up, VM), (d_hidden, VM), (convt, VM)],
        [wide, pltpu.VMEM((C, N), BF), pltpu.VMEM((3 * C, N), BF), pltpu.VMEM((3 * C, N), F32)],
        flops=1 << 30,
        mib=16,
    )
    total = (jnp.sum(parts.astype(F32), axis=0) + blank).astype(BF)
    chips = lax.axis_size(("y", "xl"))
    parts = jnp.broadcast_to(total[None], (chips, UNITS, 128))
    parts = lax.all_to_all(parts, ("y", "xl"), 0, 0, tiled=True)
    mine = jnp.sum(parts.reshape(chips // 2, 2, UNITS, 128).astype(F32), axis=0).astype(BF)
    theirs = lax.ppermute(mine, "core", [(0, 1), (1, 0)])
    conv_grad, expand_grad, project_grad = call(
        unpack_kernel,
        [
            shape(DEPTH, 8, 9 * C, dtype=F32),
            shape(DEPTH, 32, C, dtype=F32),
            shape(DEPTH, 8, HID, dtype=F32),
        ],
        [(mine, VM), (theirs, VM)],
    )
    return section_out[None], input_grad[None], conv_grad, expand_grad, project_grad


def solution(mesh):
    split = Mesh(mesh.devices.reshape(4, 2, 2, 8), LON + ("ens",))
    cells = P("ens", None, None, LON)
    rows = P(None, "ens", None)
    return jax.shard_map(
        local,
        mesh=split,
        in_specs=(cells, cells, P(), P(), P(), P(), P()),
        out_specs=(cells, cells, rows, rows, rows),
        check_vma=False,
    )
```

```python
import jax
import jax.numpy as jnp
from jax import lax
from jax.experimental import pallas as pl
from jax.experimental.pallas import tpu as pltpu
from jax.sharding import Mesh
from jax.sharding import PartitionSpec as P

BF = jnp.bfloat16
VM = pltpu.VMEM
F32 = jnp.float32
SQRT_HALF = 0.7071067811865476
INV_ROOT_TAU = 0.3989422804014327
HALF_LOG2E = 0.7213475204444817

C = 64
HID = 256
H = 8
WD = 256
HALO = 8
PITCH = WD + 2 * HALO
N = H * PITCH
DEPTH = 4
HALVES = WD // 128
TILES = N // 128
UNITS = 72
BIAS_ROWS = 16
CHUNKS = [(s, min(256, N - s)) for s in range(0, N, 256)]
FORWARD_LAG = 9
GELU_PARTS = 4
GROUP = 3
BACKWARD_LAG = 8
TURN = 8


LON = ("y", "xl", "core")

NT = (((1,), (1,)), ((), ()))


def mm(a, b):
    return jnp.dot(a, b, preferred_element_type=F32)


def mm_nt(a, b):
    return lax.dot_general(a, b, NT, preferred_element_type=F32)


def call(body, outs, ins, scratch=(), flops=0, mib=8):
    specs = [pl.BlockSpec(memory_space=space) for _, space in ins]
    return pl.pallas_call(
        body,
        out_shape=outs,
        in_specs=specs,
        out_specs=jax.tree.map(lambda _: pl.BlockSpec(memory_space=pltpu.VMEM), outs),
        scratch_shapes=list(scratch),
        compiler_params=pltpu.CompilerParams(vmem_limit_bytes=mib << 20),
        cost_estimate=pl.CostEstimate(flops=flops, bytes_accessed=1 << 20, transcendentals=0),
    )(*[array for array, _ in ins])


def shape(*dims, dtype=BF):
    return jax.ShapeDtypeStruct(dims, dtype)


def spread(wide, ref):
    for half in range(HALVES):
        part = ref[:, :, 128 * half : 128 * half + 128]
        wide[half] = part.astype(F32).reshape(C * H, 128)


def stored_row(flip, row):
    return jnp.where(flip == 1, H - 1 - row, row)


def edge_kernel(*refs):
    orient_in, *sources = refs[0:7]
    inner_ref, outer_ref, flag_ref, *targets = refs[7:16]
    wide_f, wide_g, orient_s, sems = refs[16:20]
    copies = [pltpu.make_async_copy(orient_in, orient_s, sems.at[0])]
    for i, (source, target) in enumerate(zip(sources, targets)):
        copies.append(pltpu.make_async_copy(source, target, sems.at[i + 1]))
    for copy in copies:
        copy.start()
    for copy in copies[0:3]:
        copy.wait()
    sector = (lax.axis_index("y") * 2 + lax.axis_index("xl")) * 2 + lax.axis_index("core")
    flip = orient_s[sector]
    flag_ref[...] = jnp.full((8, 128), flip, jnp.int32)
    spread(wide_f, targets[0])
    spread(wide_g, targets[1])
    lane = lax.broadcasted_iota(jnp.int32, (C, 128), 1)
    low = jnp.zeros((C, 128), F32)
    high = jnp.zeros((C, 128), F32)
    for row in range(H):
        stored = stored_row(flip, row)
        for k, wide in ((0, wide_f), (8, wide_g)):
            at = 16 * row + k
            inside = (lane >= at) & (lane < at + 8)
            first = wide[0, pl.ds(stored, C, stride=H), :]
            last = wide[HALVES - 1, pl.ds(stored, C, stride=H), :]
            low = jnp.where(inside, pltpu.roll(first, at, axis=1), low)
            high = jnp.where(inside, pltpu.roll(last, (at + 8) % 128, axis=1), high)
    first = lax.axis_index("core") == 0
    inner_ref[...] = jnp.where(first, high, low).astype(BF)
    outer_ref[...] = jnp.where(first, low, high).astype(BF)
    for copy in copies[3:]:
        copy.wait()


def flatten(ref, wide, flip):
    spread(wide, ref)
    edge = jnp.zeros((C, HALO), F32)
    parts = []
    for row in range(H):
        stored = stored_row(flip, row)
        parts.append(edge)
        for half in range(HALVES):
            parts.append(wide[half, pl.ds(stored, C, stride=H), :])
        parts.append(edge)
    return jnp.concatenate(parts, axis=1)


def unflatten(flat_ref, ref, wide, flip):
    for row in range(H):
        stored = stored_row(flip, row)
        for half in range(HALVES):
            at = row * PITCH + HALO + 128 * half
            wide[half, pl.ds(stored, C, stride=H), :] = flat_ref[:, at : at + 128].astype(F32)
    for half in range(HALVES):
        ref[:, :, 128 * half : 128 * half + 128] = wide[half].reshape(C, H, 128).astype(BF)


def prep_kernel(
    flag_ref,
    field_ref,
    slope_ref,
    kernel_ref,
    expandt_ref,
    bias_ref,
    project_ref,
    field_out,
    slope_out,
    conv_out,
    convt_out,
    expand_out,
    project_out,
    projectt_out,
    mask_out,
    wide,
):
    flip = flag_ref[0, 0]
    field_out[...] = flatten(field_ref, wide, flip).astype(BF)
    slope_out[...] = flatten(slope_ref, wide, flip).astype(BF)
    lane = lax.broadcasted_iota(jnp.int32, (16, N), 1)
    column = lane
    for row in range(1, H):
        column = jnp.where(lane >= row * PITCH, lane - row * PITCH, column)
    mask = jnp.where((column >= HALO) & (column < HALO + WD), 1.0, 0.0).astype(BF)
    for k in range(0, C, 16):
        mask_out[k : k + 16, :] = mask
    lane = lax.broadcasted_iota(jnp.int32, (HID, 128), 1)
    for b in range(DEPTH):
        taps = kernel_ref[b]
        turned = taps.astype(F32).T
        for c in range(3):
            here = slice(c * C, c * C + C)
            at = [(3 * r + c) * C for r in range(3)]
            conv_out[b, here, :] = jnp.concatenate([taps[:, a : a + C] for a in at], axis=1)
            convt_out[b, here, :] = jnp.concatenate(
                [turned[a : a + C, :] for a in at], axis=1
            ).astype(BF)
        bias = jnp.broadcast_to(bias_ref[b : b + 1, :], (128, HID)).T
        high = bias.astype(BF).astype(F32)
        middle = (bias - high).astype(BF).astype(F32)
        low = bias - high - middle
        parts = jnp.where(lane == 0, high, jnp.where(lane == 1, middle, jnp.where(lane == 2, low, 0.0)))
        weight = jnp.concatenate([expandt_ref[b].astype(F32).T, parts[:, 0:BIAS_ROWS]], axis=1)
        expand_out[b] = weight.astype(BF)
        half = 0.5 * project_ref[b].astype(F32)
        project_out[b] = half.astype(BF)
        projectt_out[b] = half.T.astype(BF)


def add_halo(flat_ref, left, right):
    lane = lax.broadcasted_iota(jnp.int32, (C, 128), 1)
    for j in range(H + 1):
        cut = slice(256 * j, 256 * j + 128)
        tile = flat_ref[:, cut].astype(F32)
        tile = jnp.where((lane >= 16 * j) & (lane < 16 * j + 8), left, tile)
        tile = jnp.where((lane >= 16 * j - 8) & (lane < 16 * j), right, tile)
        flat_ref[:, cut] = tile.astype(BF)


def shift(flat, amount):
    return pltpu.roll(flat, amount % N, axis=1)


def rows_stack(dst, value, lane, sign):
    before = jnp.where(lane < PITCH, 0, shift(value, PITCH)).astype(BF)
    after = jnp.where(lane >= N - PITCH, 0, shift(value, -PITCH)).astype(BF)
    first, last = (before, after) if sign > 0 else (after, before)
    dst[0:C, :] = first
    dst[C : 2 * C, :] = value
    dst[2 * C : 3 * C, :] = last


def conv_pass(dst, weights, src):
    for start, size in CHUNKS:
        cut = slice(start, start + size)
        dst[:, cut] = mm(weights, src[:, cut])


def pack_share(dst, at, cg, eg, pg):
    blank = jnp.zeros((8, C), F32)
    for e in range(8):
        conv = [cg[c * C + 8 * e : c * C + 8 * e + 8, :] for c in range(3)]
        wide = [eg[32 * e + 8 * i : 32 * e + 8 * i + 8, :] for i in range(4)]
        tail = [conv[i][:, 128:192] for i in range(3)] + wide + [blank]
        units = [conv[i][:, 0:128] for i in range(3)]
        units += [pg[8 * e : 8 * e + 8, 0:128], pg[8 * e : 8 * e + 8, 128:256]]
        units += [jnp.concatenate(tail[2 * i : 2 * i + 2], axis=1) for i in range(4)]
        for i, unit in enumerate(units):
            dst[at, e, 8 * i : 8 * i + 8, :] = unit


def tile(ref, t, rows=slice(None)):
    return ref[rows, 128 * t : 128 * t + 128]


def span(t):
    return slice(128 * t, 128 * t + 128)


TILE_SETS = [[t for t in range(s // 128, (s + z) // 128)] for s, z in CHUNKS]
CUTS = [slice(s, s + z) for s, z in CHUNKS]
COUNT = len(CHUNKS)


def make_row_stack(src_ref, dst_ref, sign):
    lane = lax.broadcasted_iota(jnp.int32, (C, 128), 1)
    rolled = {}

    def roll16(t, way):
        if (t, way) not in rolled:
            rolled[t, way] = pltpu.roll(tile(src_ref, t), 16 * way % 128, axis=1)
        return rolled[t, way]

    def stack(t):
        if t < 2:
            before = jnp.zeros((C, 128), BF)
        elif t == 2:
            before = jnp.where(lane < 16, 0, roll16(0, 1)).astype(BF)
        else:
            before = jnp.where(lane < 16, roll16(t - 3, 1), roll16(t - 2, 1))
        if t > TILES - 3:
            after = jnp.zeros((C, 128), BF)
        elif t == TILES - 3:
            after = jnp.where(lane < 112, roll16(TILES - 1, -1), 0).astype(BF)
        else:
            after = jnp.where(lane < 112, roll16(t + 2, -1), roll16(t + 3, -1))
        first, last = (before, after) if sign > 0 else (after, before)
        dst_ref[0:C, span(t)] = first
        dst_ref[C : 2 * C, span(t)] = tile(src_ref, t)
        dst_ref[2 * C : 3 * C, span(t)] = last

    return stack


def make_neighbours(read_right, read_left):
    lane = lax.broadcasted_iota(jnp.int32, (C, 128), 1)
    right = {}
    left = {}

    def get(t):
        for k in (t - 1, t):
            if k not in right:
                right[k] = pltpu.roll(read_right(k % TILES), 1, axis=1)
        for k in (t, t + 1):
            if k not in left:
                left[k] = pltpu.roll(read_left(k % TILES), 127, axis=1)
        return jnp.where(lane < 1, right[t - 1], right[t]), jnp.where(lane < 127, left[t], left[t + 1])

    return get


def forward_stages(
    b, out_ref, stack_s, wide_s, hid_s, active_s, slope_s, conv_ref, expand_ref, project_ref, inner_s
):
    stack = make_row_stack(out_ref, stack_s.at[b], 1)
    moved = make_neighbours(
        lambda t: tile(wide_s, t, slice(0, C)), lambda t: tile(wide_s, t, slice(2 * C, 3 * C))
    )

    def stacks(i):
        for t in TILE_SETS[i]:
            stack(t)

    def conv(i):
        wide_s[:, CUTS[i]] = mm(conv_ref[b], stack_s[b, :, CUTS[i]])

    def hidden(i):
        for t in TILE_SETS[i]:
            low, high = moved(t)
            hid_s[b, 0:C, span(t)] = (low + tile(wide_s, t, slice(C, 2 * C)) + high).astype(BF)

    def expand(i):
        cut = CUTS[i]
        inner_s[:, cut] = mm(expand_ref[b], hid_s[b, :, cut])

    def gelu(i):
        cut = CUTS[i]
        for part in range(GELU_PARTS):
            rows = slice(part * HID // GELU_PARTS, (part + 1) * HID // GELU_PARTS)
            inner = inner_s[rows, cut]
            twice = 1.0 + lax.erf(inner * SQRT_HALF)
            bell = jnp.exp2((inner * inner) * -HALF_LOG2E)
            slope_s[b, rows, cut] = (twice + (inner * (2.0 * INV_ROOT_TAU)) * bell).astype(BF)
            active_s[b, rows, cut] = (inner * twice).astype(BF)

    def project(i):
        cut = CUTS[i]
        old = stack_s[b, C : 2 * C, cut].astype(F32)
        out_ref[:, cut] = (old + mm(project_ref[b], active_s[b, :, cut])).astype(BF)

    return [(conv, 1), (gelu, 5), (expand, 4), (hidden, 3), (project, 6), (stacks, 0)]


def add_to(total, term):
    total[:] = [total[0] + term] if total else [term]


def backward_stages(
    b, up_ref, dh_ref, stack_s, rstack_s, own_s, wide_s, hid_s, active_s, slope_s, din_s, mask_s,
    convt_ref, expandt_ref, projectt_ref, sums,
):
    stack = make_row_stack(dh_ref, rstack_s, -1)
    moved = make_neighbours(
        lambda t: tile(wide_s, t, slice(2 * C, 3 * C)), lambda t: tile(wide_s, t, slice(0, C))
    )
    own_moved = make_neighbours(
        lambda t: tile(own_s, t, slice(C, 2 * C)), lambda t: tile(own_s, t, slice(C, 2 * C))
    )
    pg = []
    eg = []
    cg = []

    def inner(i):
        cut = CUTS[i]
        up = up_ref[:, cut]
        d_active = mm(projectt_ref[b], up)
        din_s[:, cut] = (d_active * slope_s[b, :, cut].astype(F32)).astype(BF)
        add_to(pg, mm_nt(up * mask_s[:, cut], active_s[b, :, cut]))

    def hidden(i):
        cut = CUTS[i]
        d_inner = din_s[:, cut]
        d_hidden = mm(expandt_ref[b], d_inner).astype(BF)
        dh_ref[:, cut] = d_hidden
        own_s[C : 2 * C, cut] = d_hidden * mask_s[:, cut]
        add_to(eg, mm_nt(d_inner, hid_s[b, 0:C, cut] * mask_s[:, cut]))

    def shares(i):
        for t in TILE_SETS[i]:
            right, left = own_moved(t)
            own_s[0:C, span(t)] = left
            own_s[2 * C : 3 * C, span(t)] = right
        if i % GROUP == GROUP - 1:
            cut = slice(CUTS[i + 1 - GROUP].start, CUTS[i].stop)
            add_to(cg, mm_nt(own_s[:, cut], stack_s[b, :, cut]))

    def stacks(i):
        for t in TILE_SETS[i]:
            stack(t)

    def conv(i):
        wide_s[:, CUTS[i]] = mm(convt_ref[b], rstack_s[:, CUTS[i]])

    def update(i):
        for t in TILE_SETS[i]:
            right, left = moved(t)
            total = tile(up_ref, t).astype(F32) + (left + tile(wide_s, t, slice(C, 2 * C)) + right)
            up_ref[:, span(t)] = total.astype(BF)

    def finish():
        sums[b] = (cg[0], eg[0], 0.5 * pg[0])

    stages = [(inner, 0), (hidden, 1), (shares, 3)]
    if b > 0:
        stages += [(stacks, 4), (conv, 5), (update, 7)]
    return stages, finish


def emit(jobs):
    last = max(first + max(lag for _, lag in stages) + COUNT for first, stages, _ in jobs)
    for step in range(last + 1):
        for first, stages, finish in jobs:
            for stage, lag in stages:
                i = step - first - lag
                if 0 <= i < COUNT:
                    stage(i)
            if finish is not None and step == first + max(lag for _, lag in stages) + COUNT:
                finish()


def main_kernel(
    field_ref,
    slope_ref,
    inner_ref,
    outer_ref,
    conv_ref,
    convt_ref,
    expand_ref,
    expandt_ref,
    project_ref,
    projectt_ref,
    mask_s,
    out_ref,
    up_ref,
    dh_ref,
    own_ref,
    other_ref,
    stack_s,
    hid_s,
    active_s,
    slope_s,
    wide_s,
    rstack_s,
    share_s,
    own_s,
    din_s,
    inner_s,
):
    core = lax.axis_index("core")
    first = core == 0
    inner = inner_ref[...].astype(F32)
    outer = outer_ref[...].astype(F32)
    left = jnp.where(first, outer, inner)
    right = jnp.where(first, inner, outer)
    out_ref[...] = field_ref[...]
    add_halo(out_ref, left, pltpu.roll(right, 8, axis=1))
    up_ref[...] = slope_ref[...]
    add_halo(up_ref, pltpu.roll(left, 120, axis=1), right)

    bias_row = lax.broadcasted_iota(jnp.int32, (BIAS_ROWS, N), 0)
    for b in range(DEPTH):
        hid_s[b, C : C + BIAS_ROWS, :] = jnp.where(bias_row < 3, 1.0, 0.0).astype(BF)
    wide_s[:, N - 128 : N] = jnp.zeros((3 * C, 128), F32)
    own_s[C : 2 * C, N - 128 : N] = jnp.zeros((C, 128), BF)
    jobs = []
    first = 0
    for b in range(DEPTH):
        stages = forward_stages(
            b, out_ref, stack_s, wide_s, hid_s, active_s, slope_s,
            conv_ref, expand_ref, project_ref, inner_s,
        )
        jobs.append((first, stages, None))
        first += FORWARD_LAG
    first = first - FORWARD_LAG + TURN
    sums = {}

    def closing(b, finish):
        def run():
            finish()
            pack_share(share_s, b, *sums[b])

        return run

    for b in reversed(range(DEPTH)):
        stages, finish = backward_stages(
            b, up_ref, dh_ref, stack_s, rstack_s, own_s, wide_s, hid_s, active_s, slope_s, din_s,
            mask_s, convt_ref, expandt_ref, projectt_ref, sums,
        )
        jobs.append((first, stages, closing(b, finish)))
        first += BACKWARD_LAG
    emit(jobs)
    own_ref[...] = share_s[pl.ds(2 * core, 2)].reshape(16 * UNITS, 128).astype(BF)
    other_ref[...] = share_s[pl.ds(2 - 2 * core, 2)].reshape(16 * UNITS, 128).astype(BF)


def step_back(up_ref, dh_ref, weights, rstack_s, wide_s, lane):
    rows_stack(rstack_s, dh_ref[...], lane, -1)
    conv_pass(wide_s, weights, rstack_s)
    up_ref[...] = (
        up_ref[...].astype(F32)
        + (shift(wide_s[0:C, :], -1) + wide_s[C : 2 * C, :] + shift(wide_s[2 * C : 3 * C, :], 1))
    ).astype(BF)


def tail_kernel(
    flag_ref, flat_ref, up_in, dh_ref, convt_ref, out_ref, grad_ref, blank_ref, wide, up_s, rstack_s, wide_s
):
    flip = flag_ref[0, 0]
    lane = lax.broadcasted_iota(jnp.int32, (C, N), 1)
    up_s[...] = up_in[...]
    step_back(up_s, dh_ref, convt_ref[0], rstack_s, wide_s, lane)
    blank_ref[...] = jnp.zeros((UNITS, 128), F32)
    unflatten(flat_ref, out_ref, wide, flip)
    unflatten(up_s, grad_ref, wide, flip)


def unpack_kernel(mine_ref, theirs_ref, conv_ref, expand_ref, project_ref):
    core = lax.axis_index("core")
    for source, pair in ((mine_ref, core), (theirs_ref, 1 - core)):
        for xl in range(2):
            unpack_block(source[xl].astype(F32), 2 * pair + xl, conv_ref, expand_ref, project_ref)


def unpack_block(total, b, conv_ref, expand_ref, project_ref):
    unit = [total[8 * i : 8 * i + 8, :] for i in range(9)]
    tail = []
    for i in range(5, 9):
        tail += [unit[i][:, 0:C], unit[i][:, C : 2 * C]]
    pieces = []
    for r in range(3):
        for c in range(3):
            pieces.append(tail[c] if r == 2 else unit[c][:, C * r : C * r + C])
    conv_ref[b] = jnp.concatenate(pieces, axis=1)
    for i in range(4):
        expand_ref[b, 8 * i : 8 * i + 8, :] = tail[3 + i]
    project_ref[b] = jnp.concatenate([unit[3], unit[4]], axis=1)


def main_scratch():
    return [
        pltpu.VMEM((DEPTH, 3 * C, N), BF),
        pltpu.VMEM((DEPTH, C + BIAS_ROWS, N), BF),
        pltpu.VMEM((DEPTH, HID, N), BF),
        pltpu.VMEM((DEPTH, HID, N), BF),
        pltpu.VMEM((3 * C, N), F32),
        pltpu.VMEM((3 * C, N), BF),
        pltpu.VMEM((DEPTH, 8, UNITS, 128), F32),
        pltpu.VMEM((3 * C, N), BF),
        pltpu.VMEM((HID, N), BF),
        pltpu.VMEM((HID, N), F32),
    ]


def local(members_in, cotangent, conv_weight, expand_weight, expand_bias, project_weight, orient):
    field = members_in[0]
    slope = cotangent[0]
    wide = pltpu.VMEM((HALVES, C * H, 128), F32)
    sources = [field, slope, conv_weight, expand_weight.transpose(0, 2, 1), expand_bias, project_weight]
    inner, outer, flag, field, slope, taps, expandt, bias, weight = call(
        edge_kernel,
        [shape(C, 128), shape(C, 128), shape(8, 128, dtype=jnp.int32)]
        + [shape(*array.shape, dtype=array.dtype) for array in sources],
        [(pltpu.with_memory_space_constraint(array, pltpu.HBM), pl.ANY) for array in [orient] + sources],
        [wide, wide, pltpu.SMEM((16,), jnp.int32), pltpu.SemaphoreType.DMA((7,))],
        mib=8,
    )
    count = lax.axis_size(LON)
    inner = lax.ppermute(inner, "core", [(0, 1), (1, 0)])
    across = [(i, (i + 1) % count) for i in range(1, count, 2)]
    outer = lax.ppermute(outer, LON, across + [(target, source) for source, target in across])

    flat_f, flat_g, conv, convt, expand, project, projectt, mask = call(
        prep_kernel,
        [
            shape(C, N),
            shape(C, N),
            shape(DEPTH, 3 * C, 3 * C),
            shape(DEPTH, 3 * C, 3 * C),
            shape(DEPTH, HID, C + BIAS_ROWS),
            shape(DEPTH, C, HID),
            shape(DEPTH, HID, C),
            shape(C, N),
        ],
        [
            (flag, VM),
            (field, VM),
            (slope, VM),
            (taps, VM),
            (expandt, VM),
            (bias, VM),
            (weight, VM),
        ],
        [wide],
        flops=1 << 27,
        mib=16,
    )
    flat_out, up, d_hidden, own, other = call(
        main_kernel,
        [
            shape(C, N),
            shape(C, N),
            shape(C, N),
            shape(16 * UNITS, 128),
            shape(16 * UNITS, 128),
        ],
        [
            (flat_f, VM),
            (flat_g, VM),
            (inner, VM),
            (outer, VM),
            (conv, VM),
            (convt, VM),
            (expand, VM),
            (expandt, VM),
            (project, VM),
            (projectt, VM),
            (mask, VM),
        ],
        main_scratch(),
        flops=1 << 33,
        mib=40,
    )
    came = lax.ppermute(other, "core", [(0, 1), (1, 0)])
    share = (own.astype(F32) + came.astype(F32)).astype(BF)
    parts = lax.all_to_all(share.reshape(16, UNITS, 128), ("xl", "ens"), 0, 0, tiled=True)
    section_out, input_grad, blank = call(
        tail_kernel,
        [shape(C, H, WD)] * 2 + [shape(UNITS, 128, dtype=F32)],
        [(flag, VM), (flat_out, VM), (up, VM), (d_hidden, VM), (convt, VM)],
        [wide, pltpu.VMEM((C, N), BF), pltpu.VMEM((3 * C, N), BF), pltpu.VMEM((3 * C, N), F32)],
        flops=1 << 30,
        mib=16,
    )
    total = (jnp.sum(parts.astype(F32), axis=0) + blank).astype(BF)
    chips = lax.axis_size(("y", "xl"))
    parts = jnp.broadcast_to(total[None], (chips, UNITS, 128))
    parts = lax.all_to_all(parts, ("y", "xl"), 0, 0, tiled=True)
    mine = jnp.sum(parts.reshape(chips // 2, 2, UNITS, 128).astype(F32), axis=0).astype(BF)
    theirs = lax.ppermute(mine, "core", [(0, 1), (1, 0)])
    conv_grad, expand_grad, project_grad = call(
        unpack_kernel,
        [
            shape(DEPTH, 8, 9 * C, dtype=F32),
            shape(DEPTH, 32, C, dtype=F32),
            shape(DEPTH, 8, HID, dtype=F32),
        ],
        [(mine, VM), (theirs, VM)],
    )
    return section_out[None], input_grad[None], conv_grad, expand_grad, project_grad


def solution(mesh):
    split = Mesh(mesh.devices.reshape(4, 2, 2, 8), LON + ("ens",))
    cells = P("ens", None, None, LON)
    rows = P(None, "ens", None)
    return jax.shard_map(
        local,
        mesh=split,
        in_specs=(cells, cells, P(), P(), P(), P(), P()),
        out_specs=(cells, cells, rows, rows, rows),
        check_vma=False,
    )
```

```python
import jax
import jax.numpy as jnp
from jax import lax
from jax.experimental import pallas as pl
from jax.experimental.pallas import tpu as pltpu
from jax.sharding import Mesh
from jax.sharding import PartitionSpec as P

BF = jnp.bfloat16
VM = pltpu.VMEM
F32 = jnp.float32
SQRT_HALF = 0.7071067811865476
INV_ROOT_TAU = 0.3989422804014327
HALF_LOG2E = 0.7213475204444817

C = 64
HID = 256
H = 8
WD = 256
HALO = 8
PITCH = WD + 2 * HALO
N = H * PITCH
DEPTH = 4
HALVES = WD // 128
TILES = N // 128
UNITS = 72
BIAS_ROWS = 16
CHUNKS = [(s, min(256, N - s)) for s in range(0, N, 256)]
FORWARD_LAG = 9
GELU_PARTS = 4
GROUP = 3
BACKWARD_LAG = 8
TURN = 8


LON = ("y", "xl", "core")

NT = (((1,), (1,)), ((), ()))


def mm(a, b):
    return jnp.dot(a, b, preferred_element_type=F32)


def mm_nt(a, b):
    return lax.dot_general(a, b, NT, preferred_element_type=F32)


def call(body, outs, ins, scratch=(), flops=0, mib=8):
    specs = [pl.BlockSpec(memory_space=space) for _, space in ins]
    return pl.pallas_call(
        body,
        out_shape=outs,
        in_specs=specs,
        out_specs=jax.tree.map(lambda _: pl.BlockSpec(memory_space=pltpu.VMEM), outs),
        scratch_shapes=list(scratch),
        compiler_params=pltpu.CompilerParams(vmem_limit_bytes=mib << 20),
        cost_estimate=pl.CostEstimate(flops=flops, bytes_accessed=1 << 20, transcendentals=0),
    )(*[array for array, _ in ins])


def shape(*dims, dtype=BF):
    return jax.ShapeDtypeStruct(dims, dtype)


def spread(wide, ref):
    for half in range(HALVES):
        part = ref[:, :, 128 * half : 128 * half + 128]
        wide[half] = part.astype(F32).reshape(C * H, 128)


def stored_row(flip, row):
    return jnp.where(flip == 1, H - 1 - row, row)


def edge_kernel(*refs):
    orient_in, *sources = refs[0:7]
    inner_ref, outer_ref, flag_ref, *targets = refs[7:16]
    wide_f, wide_g, orient_s, sems = refs[16:20]
    copies = [pltpu.make_async_copy(orient_in, orient_s, sems.at[0])]
    for i, (source, target) in enumerate(zip(sources, targets)):
        copies.append(pltpu.make_async_copy(source, target, sems.at[i + 1]))
    for copy in copies:
        copy.start()
    for copy in copies[0:3]:
        copy.wait()
    sector = (lax.axis_index("y") * 2 + lax.axis_index("xl")) * 2 + lax.axis_index("core")
    flip = orient_s[sector]
    flag_ref[...] = jnp.full((8, 128), flip, jnp.int32)
    spread(wide_f, targets[0])
    spread(wide_g, targets[1])
    lane = lax.broadcasted_iota(jnp.int32, (C, 128), 1)
    low = jnp.zeros((C, 128), F32)
    high = jnp.zeros((C, 128), F32)
    for row in range(H):
        stored = stored_row(flip, row)
        for k, wide in ((0, wide_f), (8, wide_g)):
            at = 16 * row + k
            inside = (lane >= at) & (lane < at + 8)
            first = wide[0, pl.ds(stored, C, stride=H), :]
            last = wide[HALVES - 1, pl.ds(stored, C, stride=H), :]
            low = jnp.where(inside, pltpu.roll(first, at, axis=1), low)
            high = jnp.where(inside, pltpu.roll(last, (at + 8) % 128, axis=1), high)
    first = lax.axis_index("core") == 0
    inner_ref[...] = jnp.where(first, high, low).astype(BF)
    outer_ref[...] = jnp.where(first, low, high).astype(BF)
    for copy in copies[3:]:
        copy.wait()


def flatten(ref, wide, flip):
    spread(wide, ref)
    edge = jnp.zeros((C, HALO), F32)
    parts = []
    for row in range(H):
        stored = stored_row(flip, row)
        parts.append(edge)
        for half in range(HALVES):
            parts.append(wide[half, pl.ds(stored, C, stride=H), :])
        parts.append(edge)
    return jnp.concatenate(parts, axis=1)


def unflatten(flat_ref, ref, wide, flip):
    for row in range(H):
        stored = stored_row(flip, row)
        for half in range(HALVES):
            at = row * PITCH + HALO + 128 * half
            wide[half, pl.ds(stored, C, stride=H), :] = flat_ref[:, at : at + 128].astype(F32)
    for half in range(HALVES):
        ref[:, :, 128 * half : 128 * half + 128] = wide[half].reshape(C, H, 128).astype(BF)


def prep_kernel(
    flag_ref,
    field_ref,
    slope_ref,
    kernel_ref,
    expandt_ref,
    bias_ref,
    project_ref,
    field_out,
    slope_out,
    conv_out,
    convt_out,
    expand_out,
    project_out,
    projectt_out,
    mask_out,
    wide,
):
    flip = flag_ref[0, 0]
    field_out[...] = flatten(field_ref, wide, flip).astype(BF)
    slope_out[...] = flatten(slope_ref, wide, flip).astype(BF)
    lane = lax.broadcasted_iota(jnp.int32, (16, N), 1)
    column = lane
    for row in range(1, H):
        column = jnp.where(lane >= row * PITCH, lane - row * PITCH, column)
    mask = jnp.where((column >= HALO) & (column < HALO + WD), 1.0, 0.0).astype(BF)
    for k in range(0, C, 16):
        mask_out[k : k + 16, :] = mask
    lane = lax.broadcasted_iota(jnp.int32, (HID, 128), 1)
    for b in range(DEPTH):
        taps = kernel_ref[b]
        turned = taps.astype(F32).T
        for c in range(3):
            here = slice(c * C, c * C + C)
            at = [(3 * r + c) * C for r in range(3)]
            conv_out[b, here, :] = jnp.concatenate([taps[:, a : a + C] for a in at], axis=1)
            convt_out[b, here, :] = jnp.concatenate(
                [turned[a : a + C, :] for a in at], axis=1
            ).astype(BF)
        bias = jnp.broadcast_to(bias_ref[b : b + 1, :], (128, HID)).T
        high = bias.astype(BF).astype(F32)
        middle = (bias - high).astype(BF).astype(F32)
        low = bias - high - middle
        parts = jnp.where(lane == 0, high, jnp.where(lane == 1, middle, jnp.where(lane == 2, low, 0.0)))
        weight = jnp.concatenate([expandt_ref[b].astype(F32).T, parts[:, 0:BIAS_ROWS]], axis=1)
        expand_out[b] = weight.astype(BF)
        half = 0.5 * project_ref[b].astype(F32)
        project_out[b] = half.astype(BF)
        projectt_out[b] = half.T.astype(BF)


def add_halo(flat_ref, left, right):
    lane = lax.broadcasted_iota(jnp.int32, (C, 128), 1)
    for j in range(H + 1):
        cut = slice(256 * j, 256 * j + 128)
        tile = flat_ref[:, cut].astype(F32)
        tile = jnp.where((lane >= 16 * j) & (lane < 16 * j + 8), left, tile)
        tile = jnp.where((lane >= 16 * j - 8) & (lane < 16 * j), right, tile)
        flat_ref[:, cut] = tile.astype(BF)


def shift(flat, amount):
    return pltpu.roll(flat, amount % N, axis=1)


def rows_stack(dst, value, lane, sign):
    before = jnp.where(lane < PITCH, 0, shift(value, PITCH)).astype(BF)
    after = jnp.where(lane >= N - PITCH, 0, shift(value, -PITCH)).astype(BF)
    first, last = (before, after) if sign > 0 else (after, before)
    dst[0:C, :] = first
    dst[C : 2 * C, :] = value
    dst[2 * C : 3 * C, :] = last


def conv_pass(dst, weights, src):
    for start, size in CHUNKS:
        cut = slice(start, start + size)
        dst[:, cut] = mm(weights, src[:, cut])


def pack_share(dst, at, cg, eg, pg):
    blank = jnp.zeros((8, C), F32)
    for e in range(8):
        conv = [cg[c * C + 8 * e : c * C + 8 * e + 8, :] for c in range(3)]
        wide = [eg[32 * e + 8 * i : 32 * e + 8 * i + 8, :] for i in range(4)]
        tail = [conv[i][:, 128:192] for i in range(3)] + wide + [blank]
        units = [conv[i][:, 0:128] for i in range(3)]
        units += [pg[8 * e : 8 * e + 8, 0:128], pg[8 * e : 8 * e + 8, 128:256]]
        units += [jnp.concatenate(tail[2 * i : 2 * i + 2], axis=1) for i in range(4)]
        for i, unit in enumerate(units):
            dst[at, e, 8 * i : 8 * i + 8, :] = unit


def tile(ref, t, rows=slice(None)):
    return ref[rows, 128 * t : 128 * t + 128]


def span(t):
    return slice(128 * t, 128 * t + 128)


TILE_SETS = [[t for t in range(s // 128, (s + z) // 128)] for s, z in CHUNKS]
CUTS = [slice(s, s + z) for s, z in CHUNKS]
COUNT = len(CHUNKS)


def make_row_stack(src_ref, dst_ref, sign):
    lane = lax.broadcasted_iota(jnp.int32, (C, 128), 1)
    rolled = {}

    def roll16(t, way):
        if (t, way) not in rolled:
            rolled[t, way] = pltpu.roll(tile(src_ref, t), 16 * way % 128, axis=1)
        return rolled[t, way]

    def stack(t):
        if t < 2:
            before = jnp.zeros((C, 128), BF)
        elif t == 2:
            before = jnp.where(lane < 16, 0, roll16(0, 1)).astype(BF)
        else:
            before = jnp.where(lane < 16, roll16(t - 3, 1), roll16(t - 2, 1))
        if t > TILES - 3:
            after = jnp.zeros((C, 128), BF)
        elif t == TILES - 3:
            after = jnp.where(lane < 112, roll16(TILES - 1, -1), 0).astype(BF)
        else:
            after = jnp.where(lane < 112, roll16(t + 2, -1), roll16(t + 3, -1))
        first, last = (before, after) if sign > 0 else (after, before)
        dst_ref[0:C, span(t)] = first
        dst_ref[C : 2 * C, span(t)] = tile(src_ref, t)
        dst_ref[2 * C : 3 * C, span(t)] = last

    return stack


def make_neighbours(read_right, read_left):
    lane = lax.broadcasted_iota(jnp.int32, (C, 128), 1)
    right = {}
    left = {}

    def get(t):
        for k in (t - 1, t):
            if k not in right:
                right[k] = pltpu.roll(read_right(k % TILES), 1, axis=1)
        for k in (t, t + 1):
            if k not in left:
                left[k] = pltpu.roll(read_left(k % TILES), 127, axis=1)
        return jnp.where(lane < 1, right[t - 1], right[t]), jnp.where(lane < 127, left[t], left[t + 1])

    return get


def forward_stages(
    b, out_ref, stack_s, wide_s, hid_s, active_s, slope_s, conv_ref, expand_ref, project_ref, inner_s
):
    stack = make_row_stack(out_ref, stack_s.at[b], 1)
    moved = make_neighbours(
        lambda t: tile(wide_s, t, slice(0, C)), lambda t: tile(wide_s, t, slice(2 * C, 3 * C))
    )

    def stacks(i):
        for t in TILE_SETS[i]:
            stack(t)

    def conv(i):
        wide_s[:, CUTS[i]] = mm(conv_ref[b], stack_s[b, :, CUTS[i]])

    def hidden(i):
        for t in TILE_SETS[i]:
            low, high = moved(t)
            hid_s[b, 0:C, span(t)] = (low + tile(wide_s, t, slice(C, 2 * C)) + high).astype(BF)

    def expand(i):
        cut = CUTS[i]
        inner_s[:, cut] = mm(expand_ref[b], hid_s[b, :, cut])

    def gelu(i):
        cut = CUTS[i]
        for part in range(GELU_PARTS):
            rows = slice(part * HID // GELU_PARTS, (part + 1) * HID // GELU_PARTS)
            inner = inner_s[rows, cut]
            twice = 1.0 + lax.erf(inner * SQRT_HALF)
            bell = jnp.exp2((inner * inner) * -HALF_LOG2E)
            slope_s[b, rows, cut] = (twice + (inner * (2.0 * INV_ROOT_TAU)) * bell).astype(BF)
            active_s[b, rows, cut] = (inner * twice).astype(BF)

    def project(i):
        cut = CUTS[i]
        old = stack_s[b, C : 2 * C, cut].astype(F32)
        out_ref[:, cut] = (old + mm(project_ref[b], active_s[b, :, cut])).astype(BF)

    return [(conv, 1), (gelu, 5), (expand, 4), (hidden, 3), (project, 6), (stacks, 0)]


def add_to(total, term):
    total[:] = [total[0] + term] if total else [term]


def backward_stages(
    b, up_ref, dh_ref, stack_s, rstack_s, own_s, wide_s, hid_s, active_s, slope_s, din_s, mask_s,
    convt_ref, expandt_ref, projectt_ref, sums,
):
    stack = make_row_stack(dh_ref, rstack_s, -1)
    moved = make_neighbours(
        lambda t: tile(wide_s, t, slice(2 * C, 3 * C)), lambda t: tile(wide_s, t, slice(0, C))
    )
    own_moved = make_neighbours(
        lambda t: tile(own_s, t, slice(C, 2 * C)), lambda t: tile(own_s, t, slice(C, 2 * C))
    )
    pg = []
    eg = []
    cg = []

    def inner(i):
        cut = CUTS[i]
        up = up_ref[:, cut]
        d_active = mm(projectt_ref[b], up)
        din_s[:, cut] = (d_active * slope_s[b, :, cut].astype(F32)).astype(BF)
        add_to(pg, mm_nt(up * mask_s[:, cut], active_s[b, :, cut]))

    def hidden(i):
        cut = CUTS[i]
        d_inner = din_s[:, cut]
        d_hidden = mm(expandt_ref[b], d_inner).astype(BF)
        dh_ref[:, cut] = d_hidden
        own_s[C : 2 * C, cut] = d_hidden * mask_s[:, cut]
        add_to(eg, mm_nt(d_inner, hid_s[b, 0:C, cut] * mask_s[:, cut]))

    def shares(i):
        for t in TILE_SETS[i]:
            right, left = own_moved(t)
            own_s[0:C, span(t)] = left
            own_s[2 * C : 3 * C, span(t)] = right
        if i % GROUP == GROUP - 1:
            cut = slice(CUTS[i + 1 - GROUP].start, CUTS[i].stop)
            add_to(cg, mm_nt(own_s[:, cut], stack_s[b, :, cut]))

    def stacks(i):
        for t in TILE_SETS[i]:
            stack(t)

    def conv(i):
        wide_s[:, CUTS[i]] = mm(convt_ref[b], rstack_s[:, CUTS[i]])

    def update(i):
        for t in TILE_SETS[i]:
            right, left = moved(t)
            total = tile(up_ref, t).astype(F32) + (left + tile(wide_s, t, slice(C, 2 * C)) + right)
            up_ref[:, span(t)] = total.astype(BF)

    def finish():
        sums[b] = (cg[0], eg[0], 0.5 * pg[0])

    stages = [(inner, 0), (hidden, 1), (shares, 3)]
    if b > 0:
        stages += [(stacks, 4), (conv, 5), (update, 7)]
    return stages, finish


def emit(jobs):
    last = max(first + max(lag for _, lag in stages) + COUNT for first, stages, _ in jobs)
    for step in range(last + 1):
        for first, stages, finish in jobs:
            for stage, lag in stages:
                i = step - first - lag
                if 0 <= i < COUNT:
                    stage(i)
            if finish is not None and step == first + max(lag for _, lag in stages) + COUNT:
                finish()


def main_kernel(
    field_ref,
    slope_ref,
    inner_ref,
    outer_ref,
    conv_ref,
    convt_ref,
    expand_ref,
    expandt_ref,
    project_ref,
    projectt_ref,
    mask_s,
    out_ref,
    up_ref,
    dh_ref,
    own_ref,
    other_ref,
    stack_s,
    hid_s,
    active_s,
    slope_s,
    wide_s,
    rstack_s,
    share_s,
    own_s,
    din_s,
    inner_s,
):
    core = lax.axis_index("core")
    first = core == 0
    inner = inner_ref[...].astype(F32)
    outer = outer_ref[...].astype(F32)
    left = jnp.where(first, outer, inner)
    right = jnp.where(first, inner, outer)
    out_ref[...] = field_ref[...]
    add_halo(out_ref, left, pltpu.roll(right, 8, axis=1))
    up_ref[...] = slope_ref[...]
    add_halo(up_ref, pltpu.roll(left, 120, axis=1), right)

    bias_row = lax.broadcasted_iota(jnp.int32, (BIAS_ROWS, N), 0)
    for b in range(DEPTH):
        hid_s[b, C : C + BIAS_ROWS, :] = jnp.where(bias_row < 3, 1.0, 0.0).astype(BF)
    wide_s[:, N - 128 : N] = jnp.zeros((3 * C, 128), F32)
    own_s[C : 2 * C, N - 128 : N] = jnp.zeros((C, 128), BF)
    jobs = []
    first = 0
    for b in range(DEPTH):
        stages = forward_stages(
            b, out_ref, stack_s, wide_s, hid_s, active_s, slope_s,
            conv_ref, expand_ref, project_ref, inner_s,
        )
        jobs.append((first, stages, None))
        first += FORWARD_LAG
    first = first - FORWARD_LAG + TURN
    sums = {}

    def closing(b, finish):
        def run():
            finish()
            pack_share(share_s, b, *sums[b])

        return run

    for b in reversed(range(DEPTH)):
        stages, finish = backward_stages(
            b, up_ref, dh_ref, stack_s, rstack_s, own_s, wide_s, hid_s, active_s, slope_s, din_s,
            mask_s, convt_ref, expandt_ref, projectt_ref, sums,
        )
        jobs.append((first, stages, closing(b, finish)))
        first += BACKWARD_LAG
    emit(jobs)
    own_ref[...] = share_s[pl.ds(2 * core, 2)].reshape(16 * UNITS, 128).astype(BF)
    other_ref[...] = share_s[pl.ds(2 - 2 * core, 2)].reshape(16 * UNITS, 128).astype(BF)


def step_back(up_ref, dh_ref, weights, rstack_s, wide_s, lane):
    rows_stack(rstack_s, dh_ref[...], lane, -1)
    conv_pass(wide_s, weights, rstack_s)
    up_ref[...] = (
        up_ref[...].astype(F32)
        + (shift(wide_s[0:C, :], -1) + wide_s[C : 2 * C, :] + shift(wide_s[2 * C : 3 * C, :], 1))
    ).astype(BF)


def tail_kernel(
    flag_ref, flat_ref, up_in, dh_ref, convt_ref, out_ref, grad_ref, blank_ref, wide, up_s, rstack_s, wide_s
):
    flip = flag_ref[0, 0]
    lane = lax.broadcasted_iota(jnp.int32, (C, N), 1)
    up_s[...] = up_in[...]
    step_back(up_s, dh_ref, convt_ref[0], rstack_s, wide_s, lane)
    blank_ref[...] = jnp.zeros((UNITS, 128), F32)
    unflatten(flat_ref, out_ref, wide, flip)
    unflatten(up_s, grad_ref, wide, flip)


def unpack_kernel(mine_ref, theirs_ref, conv_ref, expand_ref, project_ref):
    core = lax.axis_index("core")
    for source, pair in ((mine_ref, core), (theirs_ref, 1 - core)):
        for xl in range(2):
            unpack_block(source[xl].astype(F32), 2 * pair + xl, conv_ref, expand_ref, project_ref)


def unpack_block(total, b, conv_ref, expand_ref, project_ref):
    unit = [total[8 * i : 8 * i + 8, :] for i in range(9)]
    tail = []
    for i in range(5, 9):
        tail += [unit[i][:, 0:C], unit[i][:, C : 2 * C]]
    pieces = []
    for r in range(3):
        for c in range(3):
            pieces.append(tail[c] if r == 2 else unit[c][:, C * r : C * r + C])
    conv_ref[b] = jnp.concatenate(pieces, axis=1)
    for i in range(4):
        expand_ref[b, 8 * i : 8 * i + 8, :] = tail[3 + i]
    project_ref[b] = jnp.concatenate([unit[3], unit[4]], axis=1)


def main_scratch():
    return [
        pltpu.VMEM((DEPTH, 3 * C, N), BF),
        pltpu.VMEM((DEPTH, C + BIAS_ROWS, N), BF),
        pltpu.VMEM((DEPTH, HID, N), BF),
        pltpu.VMEM((DEPTH, HID, N), BF),
        pltpu.VMEM((3 * C, N), F32),
        pltpu.VMEM((3 * C, N), BF),
        pltpu.VMEM((DEPTH, 8, UNITS, 128), F32),
        pltpu.VMEM((3 * C, N), BF),
        pltpu.VMEM((HID, N), BF),
        pltpu.VMEM((HID, N), F32),
    ]


def local(members_in, cotangent, conv_weight, expand_weight, expand_bias, project_weight, orient):
    field = members_in[0]
    slope = cotangent[0]
    wide = pltpu.VMEM((HALVES, C * H, 128), F32)
    sources = [field, slope, conv_weight, expand_weight.transpose(0, 2, 1), expand_bias, project_weight]
    inner, outer, flag, field, slope, taps, expandt, bias, weight = call(
        edge_kernel,
        [shape(C, 128), shape(C, 128), shape(8, 128, dtype=jnp.int32)]
        + [shape(*array.shape, dtype=array.dtype) for array in sources],
        [(pltpu.with_memory_space_constraint(array, pltpu.HBM), pl.ANY) for array in [orient] + sources],
        [wide, wide, pltpu.SMEM((16,), jnp.int32), pltpu.SemaphoreType.DMA((7,))],
        mib=8,
    )
    count = lax.axis_size(LON)
    inner = lax.ppermute(inner, "core", [(0, 1), (1, 0)])
    across = [(i, (i + 1) % count) for i in range(1, count, 2)]
    outer = lax.ppermute(outer, LON, across + [(target, source) for source, target in across])

    flat_f, flat_g, conv, convt, expand, project, projectt, mask = call(
        prep_kernel,
        [
            shape(C, N),
            shape(C, N),
            shape(DEPTH, 3 * C, 3 * C),
            shape(DEPTH, 3 * C, 3 * C),
            shape(DEPTH, HID, C + BIAS_ROWS),
            shape(DEPTH, C, HID),
            shape(DEPTH, HID, C),
            shape(C, N),
        ],
        [
            (flag, VM),
            (field, VM),
            (slope, VM),
            (taps, VM),
            (expandt, VM),
            (bias, VM),
            (weight, VM),
        ],
        [wide],
        flops=1 << 27,
        mib=16,
    )
    flat_out, up, d_hidden, own, other = call(
        main_kernel,
        [
            shape(C, N),
            shape(C, N),
            shape(C, N),
            shape(16 * UNITS, 128),
            shape(16 * UNITS, 128),
        ],
        [
            (flat_f, VM),
            (flat_g, VM),
            (inner, VM),
            (outer, VM),
            (conv, VM),
            (convt, VM),
            (expand, VM),
            (expandt, VM),
            (project, VM),
            (projectt, VM),
            (mask, VM),
        ],
        main_scratch(),
        flops=1 << 33,
        mib=40,
    )
    came = lax.ppermute(other, "core", [(0, 1), (1, 0)])
    section_out, input_grad, blank = call(
        tail_kernel,
        [shape(C, H, WD)] * 2 + [shape(UNITS, 128, dtype=F32)],
        [(flag, VM), (flat_out, VM), (up, VM), (d_hidden, VM), (convt, VM)],
        [wide, pltpu.VMEM((C, N), BF), pltpu.VMEM((3 * C, N), BF), pltpu.VMEM((3 * C, N), F32)],
        flops=1 << 30,
        mib=16,
    )
    share = own.reshape(16, UNITS, 128).astype(F32) + came.reshape(16, UNITS, 128).astype(F32)
    parts = lax.all_to_all((share + blank).astype(BF), ("xl", "ens"), 0, 0, tiled=True)
    total = jnp.sum(parts.astype(F32), axis=0).astype(BF)
    chips = lax.axis_size(("y", "xl"))
    parts = jnp.broadcast_to(total[None], (chips, UNITS, 128))
    parts = lax.all_to_all(parts, ("y", "xl"), 0, 0, tiled=True)
    mine = jnp.sum(parts.reshape(chips // 2, 2, UNITS, 128).astype(F32), axis=0).astype(BF)
    theirs = lax.ppermute(mine, "core", [(0, 1), (1, 0)])
    conv_grad, expand_grad, project_grad = call(
        unpack_kernel,
        [
            shape(DEPTH, 8, 9 * C, dtype=F32),
            shape(DEPTH, 32, C, dtype=F32),
            shape(DEPTH, 8, HID, dtype=F32),
        ],
        [(mine, VM), (theirs, VM)],
    )
    return section_out[None], input_grad[None], conv_grad, expand_grad, project_grad


def solution(mesh):
    split = Mesh(mesh.devices.reshape(4, 2, 2, 8), LON + ("ens",))
    cells = P("ens", None, None, LON)
    rows = P(None, "ens", None)
    return jax.shard_map(
        local,
        mesh=split,
        in_specs=(cells, cells, P(), P(), P(), P(), P()),
        out_specs=(cells, cells, rows, rows, rows),
        check_vma=False,
    )
```

```python
import jax
import jax.numpy as jnp
from jax import lax
from jax.experimental import pallas as pl
from jax.experimental.pallas import tpu as pltpu
from jax.sharding import Mesh
from jax.sharding import PartitionSpec as P

BF = jnp.bfloat16
VM = pltpu.VMEM
F32 = jnp.float32
SQRT_HALF = 0.7071067811865476
INV_ROOT_TAU = 0.3989422804014327
HALF_LOG2E = 0.7213475204444817

C = 64
HID = 256
H = 8
WD = 256
HALO = 8
PITCH = WD + 2 * HALO
N = H * PITCH
DEPTH = 4
HALVES = WD // 128
TILES = N // 128
UNITS = 72
BIAS_ROWS = 16
CHUNKS = [(s, min(256, N - s)) for s in range(0, N, 256)]
FORWARD_LAG = 9
GELU_PARTS = 4
GROUP = 3
BACKWARD_LAG = 8
TURN = 6


LON = ("y", "xl", "core")

NT = (((1,), (1,)), ((), ()))


def mm(a, b):
    return jnp.dot(a, b, preferred_element_type=F32)


def mm_nt(a, b):
    return lax.dot_general(a, b, NT, preferred_element_type=F32)


def call(body, outs, ins, scratch=(), flops=0, mib=8):
    specs = [pl.BlockSpec(memory_space=space) for _, space in ins]
    return pl.pallas_call(
        body,
        out_shape=outs,
        in_specs=specs,
        out_specs=jax.tree.map(lambda _: pl.BlockSpec(memory_space=pltpu.VMEM), outs),
        scratch_shapes=list(scratch),
        compiler_params=pltpu.CompilerParams(vmem_limit_bytes=mib << 20),
        cost_estimate=pl.CostEstimate(flops=flops, bytes_accessed=1 << 20, transcendentals=0),
    )(*[array for array, _ in ins])


def shape(*dims, dtype=BF):
    return jax.ShapeDtypeStruct(dims, dtype)


def spread(wide, ref):
    for half in range(HALVES):
        part = ref[:, :, 128 * half : 128 * half + 128]
        wide[half] = part.astype(F32).reshape(C * H, 128)


def stored_row(flip, row):
    return jnp.where(flip == 1, H - 1 - row, row)


def edge_kernel(*refs):
    orient_in, *sources = refs[0:7]
    inner_ref, outer_ref, flag_ref, *targets = refs[7:16]
    wide_f, wide_g, orient_s, sems = refs[16:20]
    copies = [pltpu.make_async_copy(orient_in, orient_s, sems.at[0])]
    for i, (source, target) in enumerate(zip(sources, targets)):
        copies.append(pltpu.make_async_copy(source, target, sems.at[i + 1]))
    for copy in copies:
        copy.start()
    copies[1].wait()
    spread(wide_f, targets[0])
    copies[2].wait()
    spread(wide_g, targets[1])
    copies[0].wait()
    sector = (lax.axis_index("y") * 2 + lax.axis_index("xl")) * 2 + lax.axis_index("core")
    flip = orient_s[sector]
    flag_ref[...] = jnp.full((8, 128), flip, jnp.int32)
    lane = lax.broadcasted_iota(jnp.int32, (C, 128), 1)
    low = jnp.zeros((C, 128), F32)
    high = jnp.zeros((C, 128), F32)
    for row in range(H):
        stored = stored_row(flip, row)
        for k, wide in ((0, wide_f), (8, wide_g)):
            at = 16 * row + k
            inside = (lane >= at) & (lane < at + 8)
            first = wide[0, pl.ds(stored, C, stride=H), :]
            last = wide[HALVES - 1, pl.ds(stored, C, stride=H), :]
            low = jnp.where(inside, pltpu.roll(first, at, axis=1), low)
            high = jnp.where(inside, pltpu.roll(last, (at + 8) % 128, axis=1), high)
    first = lax.axis_index("core") == 0
    inner_ref[...] = jnp.where(first, high, low).astype(BF)
    outer_ref[...] = jnp.where(first, low, high).astype(BF)
    for copy in copies[3:]:
        copy.wait()


def flatten(ref, wide, flip):
    spread(wide, ref)
    edge = jnp.zeros((C, HALO), F32)
    parts = []
    for row in range(H):
        stored = stored_row(flip, row)
        parts.append(edge)
        for half in range(HALVES):
            parts.append(wide[half, pl.ds(stored, C, stride=H), :])
        parts.append(edge)
    return jnp.concatenate(parts, axis=1)


def unflatten(flat_ref, ref, wide, flip):
    for row in range(H):
        stored = stored_row(flip, row)
        for half in range(HALVES):
            at = row * PITCH + HALO + 128 * half
            wide[half, pl.ds(stored, C, stride=H), :] = flat_ref[:, at : at + 128].astype(F32)
    for half in range(HALVES):
        ref[:, :, 128 * half : 128 * half + 128] = wide[half].reshape(C, H, 128).astype(BF)


def prep_kernel(
    flag_ref,
    field_ref,
    slope_ref,
    kernel_ref,
    expandt_ref,
    bias_ref,
    project_ref,
    field_out,
    slope_out,
    conv_out,
    convt_out,
    expand_out,
    project_out,
    projectt_out,
    mask_out,
    wide,
):
    flip = flag_ref[0, 0]
    field_out[...] = flatten(field_ref, wide, flip).astype(BF)
    slope_out[...] = flatten(slope_ref, wide, flip).astype(BF)
    lane = lax.broadcasted_iota(jnp.int32, (16, N), 1)
    column = lane
    for row in range(1, H):
        column = jnp.where(lane >= row * PITCH, lane - row * PITCH, column)
    mask = jnp.where((column >= HALO) & (column < HALO + WD), 1.0, 0.0).astype(BF)
    for k in range(0, C, 16):
        mask_out[k : k + 16, :] = mask
    lane = lax.broadcasted_iota(jnp.int32, (HID, 128), 1)
    for b in range(DEPTH):
        taps = kernel_ref[b]
        turned = taps.astype(F32).T
        for c in range(3):
            here = slice(c * C, c * C + C)
            at = [(3 * r + c) * C for r in range(3)]
            conv_out[b, here, :] = jnp.concatenate([taps[:, a : a + C] for a in at], axis=1)
            convt_out[b, here, :] = jnp.concatenate(
                [turned[a : a + C, :] for a in at], axis=1
            ).astype(BF)
        bias = jnp.broadcast_to(bias_ref[b : b + 1, :], (128, HID)).T
        high = bias.astype(BF).astype(F32)
        middle = (bias - high).astype(BF).astype(F32)
        low = bias - high - middle
        parts = jnp.where(lane == 0, high, jnp.where(lane == 1, middle, jnp.where(lane == 2, low, 0.0)))
        weight = jnp.concatenate([expandt_ref[b].astype(F32).T, parts[:, 0:BIAS_ROWS]], axis=1)
        expand_out[b] = weight.astype(BF)
        half = 0.5 * project_ref[b].astype(F32)
        project_out[b] = half.astype(BF)
        projectt_out[b] = half.T.astype(BF)


def add_halo(flat_ref, left, right):
    lane = lax.broadcasted_iota(jnp.int32, (C, 128), 1)
    for j in range(H + 1):
        cut = slice(256 * j, 256 * j + 128)
        tile = flat_ref[:, cut].astype(F32)
        tile = jnp.where((lane >= 16 * j) & (lane < 16 * j + 8), left, tile)
        tile = jnp.where((lane >= 16 * j - 8) & (lane < 16 * j), right, tile)
        flat_ref[:, cut] = tile.astype(BF)


def shift(flat, amount):
    return pltpu.roll(flat, amount % N, axis=1)


def rows_stack(dst, value, lane, sign):
    before = jnp.where(lane < PITCH, 0, shift(value, PITCH)).astype(BF)
    after = jnp.where(lane >= N - PITCH, 0, shift(value, -PITCH)).astype(BF)
    first, last = (before, after) if sign > 0 else (after, before)
    dst[0:C, :] = first
    dst[C : 2 * C, :] = value
    dst[2 * C : 3 * C, :] = last


def conv_pass(dst, weights, src):
    for start, size in CHUNKS:
        cut = slice(start, start + size)
        dst[:, cut] = mm(weights, src[:, cut])


def pack_share(dst, at, cg, eg, pg):
    blank = jnp.zeros((8, C), F32)
    for e in range(8):
        conv = [cg[c * C + 8 * e : c * C + 8 * e + 8, :] for c in range(3)]
        wide = [eg[32 * e + 8 * i : 32 * e + 8 * i + 8, :] for i in range(4)]
        tail = [conv[i][:, 128:192] for i in range(3)] + wide + [blank]
        units = [conv[i][:, 0:128] for i in range(3)]
        units += [pg[8 * e : 8 * e + 8, 0:128], pg[8 * e : 8 * e + 8, 128:256]]
        units += [jnp.concatenate(tail[2 * i : 2 * i + 2], axis=1) for i in range(4)]
        for i, unit in enumerate(units):
            dst[at, e, 8 * i : 8 * i + 8, :] = unit


def tile(ref, t, rows=slice(None)):
    return ref[rows, 128 * t : 128 * t + 128]


def span(t):
    return slice(128 * t, 128 * t + 128)


TILE_SETS = [[t for t in range(s // 128, (s + z) // 128)] for s, z in CHUNKS]
CUTS = [slice(s, s + z) for s, z in CHUNKS]
COUNT = len(CHUNKS)


def make_row_stack(src_ref, dst_ref, sign):
    lane = lax.broadcasted_iota(jnp.int32, (C, 128), 1)
    rolled = {}

    def roll16(t, way):
        if (t, way) not in rolled:
            rolled[t, way] = pltpu.roll(tile(src_ref, t), 16 * way % 128, axis=1)
        return rolled[t, way]

    def stack(t):
        if t < 2:
            before = jnp.zeros((C, 128), BF)
        elif t == 2:
            before = jnp.where(lane < 16, 0, roll16(0, 1)).astype(BF)
        else:
            before = jnp.where(lane < 16, roll16(t - 3, 1), roll16(t - 2, 1))
        if t > TILES - 3:
            after = jnp.zeros((C, 128), BF)
        elif t == TILES - 3:
            after = jnp.where(lane < 112, roll16(TILES - 1, -1), 0).astype(BF)
        else:
            after = jnp.where(lane < 112, roll16(t + 2, -1), roll16(t + 3, -1))
        first, last = (before, after) if sign > 0 else (after, before)
        dst_ref[0:C, span(t)] = first
        dst_ref[C : 2 * C, span(t)] = tile(src_ref, t)
        dst_ref[2 * C : 3 * C, span(t)] = last

    return stack


def make_neighbours(read_right, read_left):
    lane = lax.broadcasted_iota(jnp.int32, (C, 128), 1)
    right = {}
    left = {}

    def get(t):
        for k in (t - 1, t):
            if k not in right:
                right[k] = pltpu.roll(read_right(k % TILES), 1, axis=1)
        for k in (t, t + 1):
            if k not in left:
                left[k] = pltpu.roll(read_left(k % TILES), 127, axis=1)
        return jnp.where(lane < 1, right[t - 1], right[t]), jnp.where(lane < 127, left[t], left[t + 1])

    return get


def forward_stages(
    b, out_ref, stack_s, wide_s, hid_s, active_s, slope_s, conv_ref, expand_ref, project_ref, inner_s
):
    stack = make_row_stack(out_ref, stack_s.at[b], 1)
    moved = make_neighbours(
        lambda t: tile(wide_s, t, slice(0, C)), lambda t: tile(wide_s, t, slice(2 * C, 3 * C))
    )

    def stacks(i):
        for t in TILE_SETS[i]:
            stack(t)

    def conv(i):
        wide_s[:, CUTS[i]] = mm(conv_ref[b], stack_s[b, :, CUTS[i]])

    def hidden(i):
        for t in TILE_SETS[i]:
            low, high = moved(t)
            hid_s[b, 0:C, span(t)] = (low + tile(wide_s, t, slice(C, 2 * C)) + high).astype(BF)

    def expand(i):
        cut = CUTS[i]
        inner_s[:, cut] = mm(expand_ref[b], hid_s[b, :, cut])

    def gelu(i):
        cut = CUTS[i]
        for part in range(GELU_PARTS):
            rows = slice(part * HID // GELU_PARTS, (part + 1) * HID // GELU_PARTS)
            inner = inner_s[rows, cut]
            twice = 1.0 + lax.erf(inner * SQRT_HALF)
            bell = jnp.exp2((inner * inner) * -HALF_LOG2E)
            slope_s[b, rows, cut] = (twice + (inner * (2.0 * INV_ROOT_TAU)) * bell).astype(BF)
            active_s[b, rows, cut] = (inner * twice).astype(BF)

    def project(i):
        cut = CUTS[i]
        old = stack_s[b, C : 2 * C, cut].astype(F32)
        out_ref[:, cut] = (old + mm(project_ref[b], active_s[b, :, cut])).astype(BF)

    return [(conv, 1), (gelu, 5), (expand, 4), (hidden, 3), (project, 6), (stacks, 0)]


def add_to(total, term):
    total[:] = [total[0] + term] if total else [term]


def backward_stages(
    b, up_ref, dh_ref, stack_s, rstack_s, own_s, wide_s, hid_s, active_s, slope_s, din_s, mask_s,
    convt_ref, expandt_ref, projectt_ref, sums,
):
    stack = make_row_stack(dh_ref, rstack_s, -1)
    moved = make_neighbours(
        lambda t: tile(wide_s, t, slice(2 * C, 3 * C)), lambda t: tile(wide_s, t, slice(0, C))
    )
    own_moved = make_neighbours(
        lambda t: tile(own_s, t, slice(C, 2 * C)), lambda t: tile(own_s, t, slice(C, 2 * C))
    )
    pg = []
    eg = []
    cg = []

    def inner(i):
        cut = CUTS[i]
        up = up_ref[:, cut]
        d_active = mm(projectt_ref[b], up)
        din_s[:, cut] = (d_active * slope_s[b, :, cut].astype(F32)).astype(BF)
        add_to(pg, mm_nt(up * mask_s[:, cut], active_s[b, :, cut]))

    def hidden(i):
        cut = CUTS[i]
        d_inner = din_s[:, cut]
        d_hidden = mm(expandt_ref[b], d_inner).astype(BF)
        dh_ref[:, cut] = d_hidden
        own_s[C : 2 * C, cut] = d_hidden * mask_s[:, cut]
        add_to(eg, mm_nt(d_inner, hid_s[b, 0:C, cut] * mask_s[:, cut]))

    def shares(i):
        for t in TILE_SETS[i]:
            right, left = own_moved(t)
            own_s[0:C, span(t)] = left
            own_s[2 * C : 3 * C, span(t)] = right
        if i % GROUP == GROUP - 1:
            cut = slice(CUTS[i + 1 - GROUP].start, CUTS[i].stop)
            add_to(cg, mm_nt(own_s[:, cut], stack_s[b, :, cut]))

    def stacks(i):
        for t in TILE_SETS[i]:
            stack(t)

    def conv(i):
        wide_s[:, CUTS[i]] = mm(convt_ref[b], rstack_s[:, CUTS[i]])

    def update(i):
        for t in TILE_SETS[i]:
            right, left = moved(t)
            total = tile(up_ref, t).astype(F32) + (left + tile(wide_s, t, slice(C, 2 * C)) + right)
            up_ref[:, span(t)] = total.astype(BF)

    def finish():
        sums[b] = (cg[0], eg[0], 0.5 * pg[0])

    stages = [(inner, 0), (hidden, 1), (shares, 3)]
    if b > 0:
        stages += [(stacks, 4), (conv, 5), (update, 7)]
    return stages, finish


def emit(jobs):
    last = max(first + max(lag for _, lag in stages) + COUNT for first, stages, _ in jobs)
    for step in range(last + 1):
        for first, stages, finish in jobs:
            for stage, lag in stages:
                i = step - first - lag
                if 0 <= i < COUNT:
                    stage(i)
            if finish is not None and step == first + max(lag for _, lag in stages) + COUNT:
                finish()


def main_kernel(
    field_ref,
    slope_ref,
    inner_ref,
    outer_ref,
    conv_ref,
    convt_ref,
    expand_ref,
    expandt_ref,
    project_ref,
    projectt_ref,
    mask_s,
    out_ref,
    up_ref,
    dh_ref,
    own_ref,
    other_ref,
    stack_s,
    hid_s,
    active_s,
    slope_s,
    wide_s,
    rstack_s,
    share_s,
    own_s,
    din_s,
    inner_s,
):
    core = lax.axis_index("core")
    first = core == 0
    inner = inner_ref[...].astype(F32)
    outer = outer_ref[...].astype(F32)
    left = jnp.where(first, outer, inner)
    right = jnp.where(first, inner, outer)
    out_ref[...] = field_ref[...]
    add_halo(out_ref, left, pltpu.roll(right, 8, axis=1))
    up_ref[...] = slope_ref[...]
    add_halo(up_ref, pltpu.roll(left, 120, axis=1), right)

    bias_row = lax.broadcasted_iota(jnp.int32, (BIAS_ROWS, N), 0)
    for b in range(DEPTH):
        hid_s[b, C : C + BIAS_ROWS, :] = jnp.where(bias_row < 3, 1.0, 0.0).astype(BF)
    wide_s[:, N - 128 : N] = jnp.zeros((3 * C, 128), F32)
    own_s[C : 2 * C, N - 128 : N] = jnp.zeros((C, 128), BF)
    jobs = []
    first = 0
    for b in range(DEPTH):
        stages = forward_stages(
            b, out_ref, stack_s, wide_s, hid_s, active_s, slope_s,
            conv_ref, expand_ref, project_ref, inner_s,
        )
        jobs.append((first, stages, None))
        first += FORWARD_LAG
    first = first - FORWARD_LAG + TURN
    sums = {}

    def closing(b, finish):
        def run():
            finish()
            pack_share(share_s, b, *sums[b])

        return run

    for b in reversed(range(DEPTH)):
        stages, finish = backward_stages(
            b, up_ref, dh_ref, stack_s, rstack_s, own_s, wide_s, hid_s, active_s, slope_s, din_s,
            mask_s, convt_ref, expandt_ref, projectt_ref, sums,
        )
        jobs.append((first, stages, closing(b, finish)))
        first += BACKWARD_LAG
    emit(jobs)
    own_ref[...] = share_s[pl.ds(2 * core, 2)].reshape(16 * UNITS, 128).astype(BF)
    other_ref[...] = share_s[pl.ds(2 - 2 * core, 2)].reshape(16 * UNITS, 128).astype(BF)


def step_back(up_ref, dh_ref, weights, rstack_s, wide_s, lane):
    rows_stack(rstack_s, dh_ref[...], lane, -1)
    conv_pass(wide_s, weights, rstack_s)
    up_ref[...] = (
        up_ref[...].astype(F32)
        + (shift(wide_s[0:C, :], -1) + wide_s[C : 2 * C, :] + shift(wide_s[2 * C : 3 * C, :], 1))
    ).astype(BF)


def tail_kernel(
    flag_ref, flat_ref, up_in, dh_ref, convt_ref, out_ref, grad_ref, blank_ref, wide, up_s, rstack_s, wide_s
):
    flip = flag_ref[0, 0]
    lane = lax.broadcasted_iota(jnp.int32, (C, N), 1)
    up_s[...] = up_in[...]
    step_back(up_s, dh_ref, convt_ref[0], rstack_s, wide_s, lane)
    blank_ref[...] = jnp.zeros((UNITS, 128), F32)
    unflatten(flat_ref, out_ref, wide, flip)
    unflatten(up_s, grad_ref, wide, flip)


def unpack_kernel(mine_ref, theirs_ref, conv_ref, expand_ref, project_ref):
    core = lax.axis_index("core")
    for source, pair in ((mine_ref, core), (theirs_ref, 1 - core)):
        for xl in range(2):
            unpack_block(source[xl].astype(F32), 2 * pair + xl, conv_ref, expand_ref, project_ref)


def unpack_block(total, b, conv_ref, expand_ref, project_ref):
    unit = [total[8 * i : 8 * i + 8, :] for i in range(9)]
    tail = []
    for i in range(5, 9):
        tail += [unit[i][:, 0:C], unit[i][:, C : 2 * C]]
    pieces = []
    for r in range(3):
        for c in range(3):
            pieces.append(tail[c] if r == 2 else unit[c][:, C * r : C * r + C])
    conv_ref[b] = jnp.concatenate(pieces, axis=1)
    for i in range(4):
        expand_ref[b, 8 * i : 8 * i + 8, :] = tail[3 + i]
    project_ref[b] = jnp.concatenate([unit[3], unit[4]], axis=1)


def main_scratch():
    return [
        pltpu.VMEM((DEPTH, 3 * C, N), BF),
        pltpu.VMEM((DEPTH, C + BIAS_ROWS, N), BF),
        pltpu.VMEM((DEPTH, HID, N), BF),
        pltpu.VMEM((DEPTH, HID, N), BF),
        pltpu.VMEM((3 * C, N), F32),
        pltpu.VMEM((3 * C, N), BF),
        pltpu.VMEM((DEPTH, 8, UNITS, 128), F32),
        pltpu.VMEM((3 * C, N), BF),
        pltpu.VMEM((HID, N), BF),
        pltpu.VMEM((HID, N), F32),
    ]


def local(members_in, cotangent, conv_weight, expand_weight, expand_bias, project_weight, orient):
    field = members_in[0]
    slope = cotangent[0]
    wide = pltpu.VMEM((HALVES, C * H, 128), F32)
    sources = [field, slope, conv_weight, expand_weight.transpose(0, 2, 1), expand_bias, project_weight]
    inner, outer, flag, field, slope, taps, expandt, bias, weight = call(
        edge_kernel,
        [shape(C, 128), shape(C, 128), shape(8, 128, dtype=jnp.int32)]
        + [shape(*array.shape, dtype=array.dtype) for array in sources],
        [(pltpu.with_memory_space_constraint(array, pltpu.HBM), pl.ANY) for array in [orient] + sources],
        [wide, wide, pltpu.SMEM((16,), jnp.int32), pltpu.SemaphoreType.DMA((7,))],
        mib=8,
    )
    count = lax.axis_size(LON)
    inner = lax.ppermute(inner, "core", [(0, 1), (1, 0)])
    across = [(i, (i + 1) % count) for i in range(1, count, 2)]
    outer = lax.ppermute(outer, LON, across + [(target, source) for source, target in across])

    flat_f, flat_g, conv, convt, expand, project, projectt, mask = call(
        prep_kernel,
        [
            shape(C, N),
            shape(C, N),
            shape(DEPTH, 3 * C, 3 * C),
            shape(DEPTH, 3 * C, 3 * C),
            shape(DEPTH, HID, C + BIAS_ROWS),
            shape(DEPTH, C, HID),
            shape(DEPTH, HID, C),
            shape(C, N),
        ],
        [
            (flag, VM),
            (field, VM),
            (slope, VM),
            (taps, VM),
            (expandt, VM),
            (bias, VM),
            (weight, VM),
        ],
        [wide],
        flops=1 << 27,
        mib=16,
    )
    flat_out, up, d_hidden, own, other = call(
        main_kernel,
        [
            shape(C, N),
            shape(C, N),
            shape(C, N),
            shape(16 * UNITS, 128),
            shape(16 * UNITS, 128),
        ],
        [
            (flat_f, VM),
            (flat_g, VM),
            (inner, VM),
            (outer, VM),
            (conv, VM),
            (convt, VM),
            (expand, VM),
            (expandt, VM),
            (project, VM),
            (projectt, VM),
            (mask, VM),
        ],
        main_scratch(),
        flops=1 << 33,
        mib=40,
    )
    came = lax.ppermute(other, "core", [(0, 1), (1, 0)])
    section_out, input_grad, blank = call(
        tail_kernel,
        [shape(C, H, WD)] * 2 + [shape(UNITS, 128, dtype=F32)],
        [(flag, VM), (flat_out, VM), (up, VM), (d_hidden, VM), (convt, VM)],
        [wide, pltpu.VMEM((C, N), BF), pltpu.VMEM((3 * C, N), BF), pltpu.VMEM((3 * C, N), F32)],
        flops=1 << 30,
        mib=16,
    )
    share = own.reshape(16, UNITS, 128).astype(F32) + came.reshape(16, UNITS, 128).astype(F32)
    parts = lax.all_to_all((share + blank).astype(BF), ("xl", "ens"), 0, 0, tiled=True)
    total = jnp.sum(parts.astype(F32), axis=0).astype(BF)
    chips = lax.axis_size(("y", "xl"))
    parts = jnp.broadcast_to(total[None], (chips, UNITS, 128))
    parts = lax.all_to_all(parts, ("y", "xl"), 0, 0, tiled=True)
    mine = jnp.sum(parts.reshape(chips // 2, 2, UNITS, 128).astype(F32), axis=0).astype(BF)
    theirs = lax.ppermute(mine, "core", [(0, 1), (1, 0)])
    conv_grad, expand_grad, project_grad = call(
        unpack_kernel,
        [
            shape(DEPTH, 8, 9 * C, dtype=F32),
            shape(DEPTH, 32, C, dtype=F32),
            shape(DEPTH, 8, HID, dtype=F32),
        ],
        [(mine, VM), (theirs, VM)],
    )
    return section_out[None], input_grad[None], conv_grad, expand_grad, project_grad


def solution(mesh):
    split = Mesh(mesh.devices.reshape(4, 2, 2, 8), LON + ("ens",))
    cells = P("ens", None, None, LON)
    rows = P(None, "ens", None)
    return jax.shard_map(
        local,
        mesh=split,
        in_specs=(cells, cells, P(), P(), P(), P(), P()),
        out_specs=(cells, cells, rows, rows, rows),
        check_vma=False,
    )
```
